128 devices in a mesh: dp: 16 (over x, z_hi, core), tensor: 8 (over z_lo, y).
Axes of the slice: x: 4, y: 4, z: 4 (z_hi: 2, z_lo: 2; z = z_hi * 2 + z_lo), core: 2. Of those that a mesh axis runs over, the one named last changes fastest.
Arguments:
- acts: bfloat16 [2, 4096, 7168], P(None, 'dp'), may hold values from -6 to 6
- counts: int32 [16, 2], P('dp'), may hold values from 0 to 256, as said below
- gate_weight: bfloat16 [7168, 2048], P('dp', 'tensor'), may hold values from -0.0625 to 0.0625
- up_weight: bfloat16 [7168, 2048], P('dp', 'tensor'), may hold values from -0.0625 to 0.0625
- down_weight: bfloat16 [7168, 2048], P('dp', 'tensor'), may hold values from -0.125 to 0.125
- out_grad: bfloat16 [2, 4096, 7168], P(None, 'dp'), may hold values from -6 to 6
Outputs:
- mixed: bfloat16 [2, 4096, 7168], P(None, 'dp', 'tensor')
- input_grad: bfloat16 [2, 4096, 7168], P(None, 'dp', 'tensor')
- gate_grad: float32 [7168, 2048], P('dp', 'tensor')
- up_grad: float32 [7168, 2048], P('dp', 'tensor')
- down_grad: float32 [7168, 2048], P('dp', 'tensor')
The draws below stay inside these ranges and needn't reach their ends.
Inputs may be any that keep to these rules, and one draw needn't show every extreme that they name: `counts`: every entry is a multiple of 128; the live rows of an index of dp in a micro-batch are its first slots; at least one entry equals 256.
All inputs are finite; a program needn't handle non-finite values.
Results may differ from the reference program's by a relative error of at most 0.02.
Values may be sent and summed in bfloat16 or wider, within the bound.
A program may use at most 128 MiB of HBM per device.

```python
import jax
import jax.numpy as jnp
from jax import lax

D = 7168
FF = 2048
ROWS = 256
BLOCK = 128
MICRO = 2
TOTAL_ROWS = 4096
N_DP = 16
N_TENSOR = 8


def draw_counts(key, part):
    key = jax.random.fold_in(key, 7)
    count_key, heavy_key, micro_key = jax.random.split(key, 3)
    block_count = jax.random.randint(count_key, (N_DP, MICRO), 0, ROWS // BLOCK + 1)
    heavy_row = jax.random.randint(heavy_key, (), 0, N_DP)
    heavy_micro = jax.random.randint(micro_key, (), 0, MICRO)
    is_full = (jnp.arange(N_DP)[:, None] == heavy_row) & (jnp.arange(MICRO)[None, :] == heavy_micro)
    block_count = jnp.where(is_full, ROWS // BLOCK, block_count)
    return (block_count * BLOCK).astype(jnp.int32)


def raised(entries, rng, source, target, shards_of, factor):
    owner, partner = [(jnp.arange(entries.shape[dim]) // (entries.shape[dim] // shards_of)).reshape([-1 if axis == dim else 1 for axis in range(entries.ndim)]) for dim in (source, target)]
    chosen = jax.random.permutation(rng, shards_of)[partner]
    strong = (owner == chosen) | (owner == (partner + shards_of // 2) % shards_of)
    return jnp.where(strong, factor * entries, entries)


def shard_levels(stream_key, dims, shards, smallest, top_value):
    factor_of = 1.0
    for dim, shards_of in shards:
        draws = jax.random.uniform(jax.random.fold_in(jax.random.fold_in(stream_key, 6), dim), (shards_of,), jnp.float32, smallest / len(shards), top_value / len(shards))
        factor_of = factor_of * jnp.repeat(jnp.exp(draws), dims[dim] // shards_of).reshape((-1,) + (1,) * (len(dims) - 1 - dim))
    return factor_of


def scatter_about(own_key, shape, spread, limit, cuts=(), kind=jnp.bfloat16):
    level = shard_levels(own_key, shape, cuts, -0.22, 0.18) if cuts else 1.0
    drawn = jax.random.normal(own_key, shape, jnp.float32) * spread * level
    return jnp.minimum(jnp.maximum(drawn, -limit), limit).astype(kind)


def noise_with(own_key, shape, scale, most, cuts, heavy, held_as=jnp.bfloat16):
    values = scale * jax.random.normal(own_key, shape, jnp.float32)
    if cuts:
        values = values * shard_levels(own_key, shape, cuts, -0.22, 0.18)
    return jnp.clip(raised(values, jax.random.fold_in(own_key, 3), *heavy), -most, most).astype(held_as)


def setup_inputs(seed: int = 0) -> dict:
    streams_of = jax.random.split(jax.random.key(seed), 7)
    acts = noise_with(streams_of[0], (MICRO, TOTAL_ROWS, D), 1.0, 6.0, ((1, 16),), (1, 2, 16, 2.0))
    counts = draw_counts(jax.random.fold_in(streams_of[6], 71), 0)
    gate_weight = scatter_about(streams_of[2], (D, FF), D ** -0.5, 0.0625, ((0, 16), (1, 8)))
    up_weight = scatter_about(streams_of[3], (D, FF), D ** -0.5, 0.0625, ((0, 16), (1, 8)))
    down_weight = scatter_about(streams_of[4], (D, FF), FF ** -0.5, 0.125, ((0, 16), (1, 8)))
    out_grad = noise_with(streams_of[5], (MICRO, TOTAL_ROWS, D), 1.0, 6.0, ((1, 16),), (1, 2, 16, 2.0))
    return dict(acts=acts, counts=counts, gate_weight=gate_weight, up_weight=up_weight, down_weight=down_weight, out_grad=out_grad)


def rounded(value):
    return lax.optimization_barrier(value.astype(jnp.bfloat16)).astype(jnp.float32)


def contract_last(left, right):
    return lax.dot_general(left, right, (((1,), (1,)), ((), ())), preferred_element_type=jnp.float32)


def reference(acts, counts, gate_weight, up_weight, down_weight, out_grad):
    micro_count = acts.shape[0]
    total_rows = acts.shape[1]
    model_width = acts.shape[2]
    slice_width = FF // N_TENSOR
    row_index = jnp.arange(total_rows, dtype=jnp.int32)
    limits = counts[row_index // ROWS]
    live_rows = ((row_index[None, :] % ROWS) < limits.T).astype(jnp.float32).reshape(-1, 1)
    flat_acts = acts.reshape(-1, model_width)
    flat_grad = out_grad.reshape(-1, model_width)

    def per_device(flat):
        shaped = flat.reshape(micro_count, N_DP, ROWS, flat.shape[1]).transpose(1, 0, 2, 3)
        return shaped.reshape(N_DP, micro_count * ROWS, flat.shape[1]).astype(jnp.float32)

    device_acts = per_device(flat_acts)
    device_grad = per_device(flat_grad)

    def group_step(carry, group):
        mixed_acc, input_acc = carry
        start = (group * slice_width).astype(jnp.int32)
        w_gate = lax.dynamic_slice_in_dim(gate_weight, start, slice_width, 1)
        w_up = lax.dynamic_slice_in_dim(up_weight, start, slice_width, 1)
        w_down = lax.dynamic_slice_in_dim(down_weight, start, slice_width, 1)
        gate_pre = jnp.dot(flat_acts, w_gate, preferred_element_type=jnp.float32)
        up_pre = jnp.dot(flat_acts, w_up, preferred_element_type=jnp.float32)
        sigma = jax.nn.sigmoid(gate_pre)
        activated = gate_pre * sigma
        hidden = (live_rows * activated * up_pre).astype(jnp.bfloat16)
        mixed_acc = mixed_acc + rounded(contract_last(hidden, w_down))
        grad_hidden = jnp.dot(flat_grad, w_down, preferred_element_type=jnp.float32)
        slope = sigma * (1.0 + gate_pre * (1.0 - sigma))
        grad_gate_pre = (live_rows * grad_hidden * up_pre * slope).astype(jnp.bfloat16)
        grad_up_pre = (live_rows * grad_hidden * activated).astype(jnp.bfloat16)
        input_term = contract_last(grad_gate_pre, w_gate) + contract_last(grad_up_pre, w_up)
        input_acc = input_acc + rounded(input_term)
        gate_part = jnp.einsum("nrd,nrf->ndf", device_acts, per_device(grad_gate_pre))
        up_part = jnp.einsum("nrd,nrf->ndf", device_acts, per_device(grad_up_pre))
        down_part = jnp.einsum("nrd,nrf->ndf", device_grad, per_device(hidden))
        sums = (jnp.sum(rounded(gate_part), axis=0), jnp.sum(rounded(up_part), axis=0), jnp.sum(rounded(down_part), axis=0))
        return (mixed_acc, input_acc), sums

    zero_rows = jnp.zeros((flat_acts.shape[0], model_width), jnp.float32)
    carry, stacked = lax.scan(group_step, (zero_rows, zero_rows), jnp.arange(N_TENSOR, dtype=jnp.int32))
    mixed_acc, input_acc = carry

    def stitch(parts):
        return parts.transpose(1, 0, 2).reshape(model_width, FF)

    mixed = mixed_acc.reshape(acts.shape).astype(jnp.bfloat16)
    input_grad = input_acc.reshape(acts.shape).astype(jnp.bfloat16)
    return mixed, input_grad, stitch(stacked[0]), stitch(stacked[1]), stitch(stacked[2])
```

```python
import jax
import jax.numpy as jnp
from jax import lax
from jax.experimental import pallas as pl
from jax.experimental.pallas import tpu as pltpu
from jax.sharding import PartitionSpec as P

MESH = pl.DeviceIdType.MESH
GATE, UP, DOWN = 0, 1, 2
HIDDEN, GGP, GUP = 0, 1, 2
SHARD = 448
CHIP = 2 * SHARD
HALF = SHARD // 2
WIDTH = 256
ROWS = 512
MICRO_ROWS = 256


def aligned(index, size, unit):
    return pl.ds(pl.multiple_of(index * unit, unit), size)


def contract_last(left, right):
    return lax.dot_general(left, right, (((1,), (1,)), ((), ())), preferred_element_type=jnp.float32)


def contract_first(left, right):
    return lax.dot_general(left, right, (((0,), (0,)), ((), ())), preferred_element_type=jnp.float32)


def kernel(
    acts, counts, gate_w, up_w, down_w, out_grad,
    mixed, input_grad, gate_grad, up_grad, down_grad,
    av, ov, wf, w2, af, rs, rx, rz, pre, fin, res,
    load_sem, own_sem, a_send, a_recv, t_send, t_recv, u_send, u_recv,
    g_send, g_recv, b_send, b_recv, out_sem,
):
    dp, t = lax.axis_index("dp"), lax.axis_index("tensor")
    x, zh, c = dp // 4, (dp // 2) % 2, dp % 2
    zl, y = t // 4, t % 4
    weights = (gate_w, up_w, down_w)

    def device(dx=0, flip_zh=0, flip_c=0, flip_zl=0, dy=0):
        return (
            ((x + dx) % 4) * 4 + ((zh + flip_zh) % 2) * 2 + (c + flip_c) % 2,
            ((zl + flip_zl) % 2) * 4 + (y + dy) % 4,
        )

    def chip_of(r):
        return ((x + r % 4) % 4) * 2 + (zh + r // 4) % 2

    def remote(src, dst, send, recv, to):
        return pltpu.make_async_remote_copy(src, dst, send, recv, device_id=to, device_id_type=MESH)

    sibling = device(flip_c=1)
    across = device(flip_zh=1)
    my_cols = aligned(t, WIDTH, WIDTH)

    barrier = pltpu.get_barrier_semaphore()
    partners = [sibling, across] + [device(dx=j) for j in (1, 2, 3)]
    partners += [device(dy=j) for j in (1, 2, 3)]
    partners += [device(flip_zl=1, dy=j) for j in range(4)]
    partners += [device(flip_zl=1, flip_zh=1, dy=j) for j in range(4)]
    for to in partners:
        pl.semaphore_signal(barrier, inc=1, device_id=to, device_id_type=MESH)

    own = [pltpu.make_async_copy(weights[w], wf.at[w, aligned(dp, SHARD, SHARD)], own_sem.at[w]) for w in range(3)]
    for copy in own:
        copy.start()
    loads = []
    for which, (src, dst) in enumerate(((acts, av), (out_grad, ov))):
        for m in range(2):
            loads.append(
                pltpu.make_async_copy(
                    src.at[m], dst.at[pl.ds(m * MICRO_ROWS, MICRO_ROWS)], load_sem.at[2 * which + m]
                )
            )
    for copy in loads:
        copy.start()
    pl.semaphore_wait(barrier, len(partners))

    sends = {w: [] for w in range(3)}

    def shard_ref(w, r, core):
        return wf.at[w, aligned(chip_of(r) * 2 + core, SHARD, SHARD)]

    def move(w, r, to, send_index, recv_index, core=None):
        ref = shard_ref(w, r, c if core is None else core)
        copy = remote(ref, ref, a_send.at[w, send_index], a_recv.at[w, recv_index], to)
        copy.start()
        sends[w].append(copy)

    def wait_shard(w, r, core, index):
        ref = shard_ref(w, r, core)
        remote(ref, ref, a_send.at[w, index], a_recv.at[w, index], sibling).wait_recv()

    def transpose_parts(w, r, act):
        d = chip_of(r)
        to_zl, to_y = d // 4, d % 4
        cross = (to_zl + zl) % 2
        for h in range(2):
            src = wf.at[w, pl.ds(pl.multiple_of((d * 2 + c) * SHARD + h * HALF, HALF), HALF)]
            dst = w2.at[w, pl.ds(pl.multiple_of(c * SHARD + h * HALF, HALF), HALF), my_cols]
            to = (x * 4 + ((zh + h * cross) % 2) * 2 + c, d)

            @pl.when(d != t)
            def _():
                act[0](remote(src, dst, t_send.at[w, r, h], t_recv.at[w, t, h], to))

            @pl.when(d == t)
            def _():
                act[1](pltpu.make_async_copy(src, dst, t_send.at[w, r, h]))

    def start(copy):
        copy.start()

    def transpose_out(w, r):
        transpose_parts(w, r, (start, start))

    def pass_on(w, r):
        move(w, r, sibling, 8 + r, 8 + r)
        transpose_out(w, r)

    def send_own(w):
        own[w].wait()
        move(w, 0, across, 4, 4)
        for j in (1, 3, 2):
            move(w, 0, device(dx=j), j, 4 - j)
        pass_on(w, 0)

    def from_across(w):
        wait_shard(w, 4, c, 4)
        for j in (1, 3, 2):
            move(w, 4, device(dx=j), 4 + j, 8 - j)
        pass_on(w, 4)

    def from_x(w, base):
        for k in (1, 3, 2):
            wait_shard(w, base + k, c, base + k)
            pass_on(w, base + k)

    def from_sibling(w, relations):
        for r in relations:
            wait_shard(w, r, 1 - c, 8 + r)

    def accumulate(which, values, relations, step, first=False):
        @pl.loop(0, len(relations))
        def _(i):
            d = chip_of(relations[0] + i * step)
            cols = aligned(d, CHIP, CHIP)
            left = values[:, cols]
            for w in which:
                part = jnp.dot(left, wf[w, cols], preferred_element_type=jnp.float32)
                if first:
                    @pl.when(i == 0)
                    def _():
                        pre[w] = part

                    @pl.when(i > 0)
                    def _():
                        pre[w] += part
                else:
                    pre[w] += part

    def live_rows(i, size):
        per = MICRO_ROWS // size
        row = lax.broadcasted_iota(jnp.int32, (size, WIDTH), 0) + (i % per) * size
        return (row < counts[0, i // per]).astype(jnp.float32)

    TILE = 64

    def gather_out(a):
        block = af.at[a, :, my_cols]
        out = [remote(block, block, g_send.at[a, 0], g_recv.at[a, 0], device(flip_zl=1))]
        for j in (1, 3, 2):
            out.append(remote(block, block, g_send.at[a, j], g_recv.at[a, 4 - j], device(dy=j)))
        for copy in out:
            copy.start()
        return out

    def group(flip_zl, k):
        return aligned(((zl + flip_zl) % 2) * 4 + (y + k) % 4, WIDTH, WIDTH)

    def gather_forward(a):
        out = []
        block = af.at[a, :, group(1, 0)]
        remote(block, block, g_send.at[a, 0], g_recv.at[a, 0], sibling).wait_recv()
        part = af.at[a, pl.ds(MICRO_ROWS, MICRO_ROWS), group(1, 0)]
        for j in (1, 3, 2):
            copy = remote(part, part, g_send.at[a, 6 + j], g_recv.at[a, 10 - j], device(dy=j))
            copy.start()
            out.append(copy)
        for k in (1, 3, 2):
            block = af.at[a, :, group(0, k)]
            remote(block, block, g_send.at[a, k], g_recv.at[a, k], sibling).wait_recv()
            part = af.at[a, pl.ds(0, MICRO_ROWS), group(0, k)]
            copy = remote(part, part, g_send.at[a, 3 + k], g_recv.at[a, 3 + k], device(flip_zl=1))
            copy.start()
            out.append(copy)
        return out

    def gather_done(a):
        for k in (1, 3, 2):
            first = af.at[a, pl.ds(0, MICRO_ROWS), group(1, k)]
            remote(first, first, g_send.at[a, 3 + k], g_recv.at[a, 3 + k], sibling).wait_recv()
            second = af.at[a, pl.ds(MICRO_ROWS, MICRO_ROWS), group(1, k)]
            remote(second, second, g_send.at[a, 6 + k], g_recv.at[a, 6 + k], sibling).wait_recv()

    def finish_weight_sends(w):
        for copy in sends[w]:
            copy.wait_send()
        for r in range(8):
            transpose_parts(w, r, (lambda copy: copy.wait_send(), lambda copy: copy.wait()))

    def columns_arrived(w):
        for f in range(8):
            for h in range(2):
                dst = w2.at[
                    w, pl.ds(pl.multiple_of(c * SHARD + h * HALF, HALF), HALF), pl.ds(f * WIDTH, WIDTH)
                ]

                @pl.when(t != f)
                def _():
                    remote(dst, dst, t_send.at[w, f, h], t_recv.at[w, f, h], sibling).wait_recv()

        mine = w2.at[w, aligned(c, SHARD, SHARD)]
        copy = remote(mine, mine, u_send.at[w], u_recv.at[w], sibling)
        copy.start()
        return copy

    def columns_done(w):
        theirs = w2.at[w, aligned(1 - c, SHARD, SHARD)]
        remote(theirs, theirs, u_send.at[w], u_recv.at[w], sibling).wait_recv()

    place = {DOWN: GATE, GATE: UP, UP: DOWN}

    def dest(i):
        return ((x + 1 + i // 2) % 4) * 2 + i % 2

    def block_of(p, i, core):
        return wf.at[place[p], aligned(dest(i) * 2 + core, SHARD, SHARD)]

    def pair_copy(p, i):
        return remote(block_of(p, i, 1 - c), rs.at[p, i], b_send.at[p, i], b_recv.at[p, i], sibling)

    def grad_partials(p, values, a):
        @pl.loop(0, 8)
        def _(i):
            d = dest(i)
            part = contract_first(values[:, aligned(d, CHIP, CHIP)], af[a, :, my_cols])
            wf[place[p], aligned(d, CHIP, CHIP)] = part.astype(jnp.bfloat16)
            pair_copy(p, i).start()

    def x_copy(p, i):
        j, half = i // 2 + 1, i % 2
        slot = (3 - j) * 2 + half
        return remote(
            block_of(p, i, c), rx.at[p, slot], b_send.at[p, 8 + i], b_recv.at[p, 8 + slot], device(dx=j)
        )

    STEP = 112

    def pair_sums(p):
        q = place[p]
        for i in range(6):
            pair_copy(p, i).wait_recv()
            base = (dest(i) * 2 + c) * SHARD

            @pl.loop(0, SHARD // STEP)
            def _(s):
                rows = pl.ds(pl.multiple_of(base + s * STEP, 16), STEP)
                total = wf[q, rows].astype(jnp.float32) + rs[p, i, aligned(s, STEP, STEP)].astype(jnp.float32)
                wf[q, rows] = total.astype(jnp.bfloat16)

            x_copy(p, i).start()

    def z_copy(p):
        src = wf.at[place[p], aligned((x * 2 + 1 - zh) * 2 + c, SHARD, SHARD)]
        return remote(src, rz.at[p], b_send.at[p, 14], b_recv.at[p, 14], across)

    def x_sums(p):
        q = place[p]
        for i in (6, 7):
            pair_copy(p, i).wait_recv()
        for slot in range(6):
            remote(
                rx.at[p, slot], rx.at[p, slot], b_send.at[p, 8 + slot], b_recv.at[p, 8 + slot], sibling
            ).wait_recv()

        def total(half, s):
            rows = pl.ds(pl.multiple_of(((x * 2 + half) * 2 + c) * SHARD + s * STEP, 16), STEP)
            inner = aligned(s, STEP, STEP)
            value = wf[q, rows].astype(jnp.float32) + rs[p, 6 + half, inner].astype(jnp.float32)
            for k in range(3):
                value += rx[p, 2 * k + half, inner].astype(jnp.float32)
            return rows, value

        @pl.loop(0, SHARD // STEP)
        def _(s):
            rows, value = total(1 - zh, s)
            wf[q, rows] = value.astype(jnp.bfloat16)

        z_copy(p).start()

        @pl.loop(0, SHARD // STEP)
        def _(s):
            rows, value = total(zh, s)
            fin[p, aligned(s, STEP, STEP)] = value

    grads = {GATE: gate_grad, UP: up_grad, DOWN: down_grad}

    def z_sums(p):
        z_copy(p).wait_recv()

        @pl.loop(0, SHARD // STEP)
        def _(s):
            inner = aligned(s, STEP, STEP)
            fin[p, inner] += rz[p, inner].astype(jnp.float32)

        copy = pltpu.make_async_copy(fin.at[p], grads[p], out_sem.at[p])
        copy.start()
        return copy

    def write_out(ref, which):
        copies = []
        for m in range(2):
            copy = pltpu.make_async_copy(
                res.at[which, pl.ds(m * MICRO_ROWS, MICRO_ROWS)], ref.at[m], out_sem.at[3 + 2 * which + m]
            )
            copy.start()
            copies.append(copy)
        return copies

    OUT_TILE = 128

    send_own(GATE)
    send_own(UP)
    from_across(GATE)
    from_across(UP)
    send_own(DOWN)
    from_x(GATE, 0)
    from_x(UP, 0)
    for copy in loads[:2]:
        copy.wait()
    for w in (GATE, UP):
        from_sibling(w, (0, 4))
    accumulate((GATE, UP), av, (0, 4), 4, first=True)
    from_across(DOWN)
    from_x(GATE, 4)
    from_x(UP, 4)
    for w in (GATE, UP):
        from_sibling(w, (1, 2, 3))
    accumulate((GATE, UP), av, (1, 2, 3), 1)
    for w in (GATE, UP):
        from_sibling(w, (5, 6, 7))
    accumulate((GATE, UP), av, (5, 6, 7), 1)

    @pl.loop(0, ROWS // TILE)
    def _(i):
        rows = aligned(i, TILE, TILE)
        gate_pre, up_pre = pre[GATE, rows], pre[UP, rows]
        value = live_rows(i, TILE) * (gate_pre * jax.nn.sigmoid(gate_pre)) * up_pre
        af[HIDDEN, rows, my_cols] = value.astype(jnp.bfloat16)

    gathers = gather_out(HIDDEN)
    from_x(DOWN, 0)
    for copy in loads[2:]:
        copy.wait()
    finish_weight_sends(GATE)
    grad_partials(DOWN, ov, HIDDEN)
    from_sibling(DOWN, (0, 4))
    accumulate((DOWN,), ov, (0, 4), 4, first=True)
    from_x(DOWN, 4)
    from_sibling(DOWN, (1, 2, 3))
    accumulate((DOWN,), ov, (1, 2, 3), 1)
    pair_sums(DOWN)
    from_sibling(DOWN, (5, 6, 7))
    accumulate((DOWN,), ov, (5, 6, 7), 1)

    @pl.loop(0, ROWS // TILE)
    def _(i):
        rows = aligned(i, TILE, TILE)
        gate_pre, up_pre, grad_hidden = pre[GATE, rows], pre[UP, rows], pre[DOWN, rows]
        sigma = jax.nn.sigmoid(gate_pre)
        scaled = live_rows(i, TILE) * grad_hidden
        slope = sigma * (1.0 + gate_pre * (1.0 - sigma))
        af[GGP, rows, my_cols] = (scaled * up_pre * slope).astype(jnp.bfloat16)
        af[GUP, rows, my_cols] = (scaled * (gate_pre * sigma)).astype(jnp.bfloat16)

    gathers += gather_out(GGP)
    gathers += gather_out(GUP)
    finish_weight_sends(UP)
    grad_partials(GATE, av, GGP)
    finish_weight_sends(DOWN)
    grad_partials(UP, av, GUP)
    gathers += gather_forward(HIDDEN)
    pair_sums(GATE)
    pair_sums(UP)
    columns = [columns_arrived(DOWN)]
    gathers += gather_forward(GGP)
    gathers += gather_forward(GUP)
    columns.append(columns_arrived(GATE))
    columns.append(columns_arrived(UP))
    x_sums(DOWN)
    gather_done(HIDDEN)
    columns_done(DOWN)

    @pl.loop(0, ROWS // OUT_TILE)
    def _(i):
        rows = aligned(i, OUT_TILE, OUT_TILE)
        res[0, rows] = contract_last(af[HIDDEN, rows], w2[DOWN]).astype(jnp.bfloat16)

    outs = write_out(mixed, 0)
    outs.append(z_sums(DOWN))
    x_sums(GATE)
    x_sums(UP)
    gather_done(GGP)
    gather_done(GUP)
    columns_done(GATE)
    columns_done(UP)

    @pl.loop(0, ROWS // OUT_TILE)
    def _(i):
        rows = aligned(i, OUT_TILE, OUT_TILE)
        value = contract_last(af[GGP, rows], w2[GATE]) + contract_last(af[GUP, rows], w2[UP])
        res[1, rows] = value.astype(jnp.bfloat16)

    outs += write_out(input_grad, 1)
    outs.append(z_sums(GATE))
    outs.append(z_sums(UP))
    for copy in gathers + columns:
        copy.wait_send()
    for p in range(3):
        for i in range(8):
            pair_copy(p, i).wait_send()
        for i in range(6):
            x_copy(p, i).wait_send()
        z_copy(p).wait_send()
    for copy in outs:
        copy.wait()


def local(acts, counts, gate_weight, up_weight, down_weight, out_grad):
    bf16, f32 = jnp.bfloat16, jnp.float32
    dma = pltpu.SemaphoreType.DMA
    anywhere = pl.BlockSpec(memory_space=pl.ANY)
    piece = jax.ShapeDtypeStruct((2, MICRO_ROWS, CHIP), bf16)
    grad = jax.ShapeDtypeStruct((SHARD, WIDTH), f32)
    return pl.pallas_call(
        kernel,
        name="expert_layer",
        out_shape=(piece, piece, grad, grad, grad),
        in_specs=[anywhere, pl.BlockSpec(memory_space=pltpu.SMEM)] + [anywhere] * 4,
        out_specs=(anywhere,) * 5,
        scratch_shapes=[
            pltpu.VMEM((ROWS, 8 * CHIP), bf16),
            pltpu.VMEM((ROWS, 8 * CHIP), bf16),
            pltpu.VMEM((3, 8 * CHIP, WIDTH), bf16),
            pltpu.VMEM((3, CHIP, 8 * WIDTH), bf16),
            pltpu.VMEM((3, ROWS, 8 * WIDTH), bf16),
            pltpu.VMEM((3, 8, SHARD, WIDTH), bf16),
            pltpu.VMEM((3, 6, SHARD, WIDTH), bf16),
            pltpu.VMEM((3, SHARD, WIDTH), bf16),
            pltpu.VMEM((3, ROWS, WIDTH), f32),
            pltpu.VMEM((3, SHARD, WIDTH), f32),
            pltpu.VMEM((2, ROWS, CHIP), bf16),
            dma((4,)),
            dma((3,)),
            dma((3, 16)),
            dma((3, 16)),
            dma((3, 8, 2)),
            dma((3, 8, 2)),
            dma((3,)),
            dma((3,)),
            dma((3, 10)),
            dma((3, 10)),
            dma((3, 15)),
            dma((3, 15)),
            dma((7,)),
        ],
        compiler_params=pltpu.CompilerParams(
            collective_id=0, has_side_effects=True, vmem_limit_bytes=62 * 2**20
        ),
    )(acts, counts, gate_weight, up_weight, down_weight, out_grad)


def solution(mesh):
    placed = (
        P(None, "dp", None),
        P("dp", None),
        P("dp", "tensor"),
        P("dp", "tensor"),
        P("dp", "tensor"),
        P(None, "dp", None),
    )
    return jax.shard_map(
        local,
        mesh=mesh,
        in_specs=placed,
        out_specs=(
            P(None, "dp", "tensor"),
            P(None, "dp", "tensor"),
            P("dp", "tensor"),
            P("dp", "tensor"),
            P("dp", "tensor"),
        ),
        check_vma=False,
    )
```

```python
import jax
import jax.numpy as jnp
from jax import lax
from jax.experimental import pallas as pl
from jax.experimental.pallas import tpu as pltpu
from jax.sharding import PartitionSpec as P

MESH = pl.DeviceIdType.MESH
GATE, UP, DOWN = 0, 1, 2
HIDDEN, GGP, GUP = 0, 1, 2
SHARD = 448
CHIP = 2 * SHARD
HALF = SHARD // 2
PAIR = 2 * CHIP
WIDTH = 256
ROWS = 512
MICRO_ROWS = 256


def aligned(index, size, unit):
    return pl.ds(pl.multiple_of(index * unit, unit), size)


def contract_last(left, right):
    return lax.dot_general(left, right, (((1,), (1,)), ((), ())), preferred_element_type=jnp.float32)


def contract_first(left, right):
    return lax.dot_general(left, right, (((0,), (0,)), ((), ())), preferred_element_type=jnp.float32)


def kernel(
    acts, counts, gate_w, up_w, down_w, out_grad,
    mixed, input_grad, gate_grad, up_grad, down_grad,
    av, ov, wf, w2, af, rs, rx, rz, pre, acc,
    load_sem, own_sem, a_send, a_recv, t_send, t_recv, u_send, u_recv,
    g_send, g_recv, b_send, b_recv, out_sem,
):
    dp, t = lax.axis_index("dp"), lax.axis_index("tensor")
    x, zh, c = dp // 4, (dp // 2) % 2, dp % 2
    zl, y = t // 4, t % 4
    my_chip = x * 2 + zh
    weights = (gate_w, up_w, down_w)

    def device(dx=0, flip_zh=0, flip_c=0, flip_zl=0, dy=0):
        return (
            ((x + dx) % 4) * 4 + ((zh + flip_zh) % 2) * 2 + (c + flip_c) % 2,
            ((zl + flip_zl) % 2) * 4 + (y + dy) % 4,
        )

    def chip_of(r):
        return ((x + r % 4) % 4) * 2 + (zh + r // 4) % 2

    def remote(src, dst, send, recv, to):
        return pltpu.make_async_remote_copy(src, dst, send, recv, device_id=to, device_id_type=MESH)

    sibling = device(flip_c=1)
    across = device(flip_zh=1)
    my_cols = aligned(t, WIDTH, WIDTH)

    barrier = pltpu.get_barrier_semaphore()
    partners = [sibling, across] + [device(dx=j) for j in (1, 2, 3)]
    partners += [device(dy=j) for j in (1, 2, 3)]
    partners += [device(flip_zl=1, dy=j) for j in range(4)]
    partners += [device(flip_zl=1, flip_zh=1, dy=j) for j in range(4)]
    for to in partners:
        pl.semaphore_signal(barrier, inc=1, device_id=to, device_id_type=MESH)

    own = [pltpu.make_async_copy(weights[w], wf.at[w, aligned(dp, SHARD, SHARD)], own_sem.at[w]) for w in range(3)]
    for copy in own:
        copy.start()
    loads = []
    for which, (src, dst) in enumerate(((acts, av), (out_grad, ov))):
        for m in range(2):
            loads.append(
                pltpu.make_async_copy(
                    src.at[m], dst.at[pl.ds(m * MICRO_ROWS, MICRO_ROWS)], load_sem.at[2 * which + m]
                )
            )
    for copy in loads:
        copy.start()
    pl.semaphore_wait(barrier, len(partners))

    sends = {w: [] for w in range(3)}

    def shard_rows(r, core, low=0, size=SHARD):
        return pl.ds(pl.multiple_of((chip_of(r) * 2 + core) * SHARD + low, HALF), size)

    def move(w, r, to, index, low=0, size=SHARD):
        ref = wf.at[w, shard_rows(r, c, low, size)]
        copy = remote(ref, ref, a_send.at[w, index], a_recv.at[w, index], to)
        copy.start()
        sends[w].append(copy)

    def arrived(w, r, index, low=0, size=SHARD, core=None):
        ref = wf.at[w, shard_rows(r, c if core is None else core, low, size)]
        remote(ref, ref, a_send.at[w, index], a_recv.at[w, index], sibling).wait_recv()

    def to_sibling(w, r):
        move(w, r, sibling, 9 + r)

    def send_own(w):
        move(w, 0, across, 0)
        move(w, 0, device(dx=1), 1)
        move(w, 0, device(dx=3), 2)
        to_sibling(w, 0)

    def from_across(w):
        arrived(w, 4, 0)
        move(w, 4, device(dx=1), 3)
        move(w, 4, device(dx=3), 4)
        to_sibling(w, 4)

    def from_neighbours(w, flip):
        arrived(w, 4 * flip + 1, 2 + 2 * flip)
        move(w, 4 * flip + 1, device(dx=3), 5 + 2 * flip, 0, HALF)
        to_sibling(w, 4 * flip + 1)
        arrived(w, 4 * flip + 3, 1 + 2 * flip)
        move(w, 4 * flip + 3, device(dx=1), 6 + 2 * flip, HALF, HALF)
        to_sibling(w, 4 * flip + 3)

    def from_far(w, flip):
        arrived(w, 4 * flip + 2, 5 + 2 * flip, 0, HALF)
        arrived(w, 4 * flip + 2, 6 + 2 * flip, HALF, HALF)
        to_sibling(w, 4 * flip + 2)

    def from_sibling(w):
        for r in range(8):
            arrived(w, r, 9 + r, core=1 - c)

    def column_copy(w, to, cross, h):
        src = wf.at[w, pl.ds(pl.multiple_of((to * 2 + c) * SHARD + h * HALF, HALF), HALF)]
        dst = w2.at[w, pl.ds(pl.multiple_of(c * SHARD + h * HALF, HALF), HALF), my_cols]
        where = (x * 4 + ((zh + h * cross) % 2) * 2 + c, to)
        return remote(src, dst, t_send.at[w, to, h], t_recv.at[w, t, h], where)

    def column_stay(w):
        src = wf.at[w, pl.ds(pl.multiple_of((t * 2 + c) * SHARD, SHARD), SHARD)]
        return pltpu.make_async_copy(src, w2.at[w, aligned(c, SHARD, SHARD), my_cols], t_send.at[w, t, 0])

    ROTATION = ((0, 1), (1, 0), (0, 3), (1, 1), (0, 2), (1, 3), (1, 2))

    def column_target(flip, j):
        return ((zl + flip) % 2) * 4 + (y + j) % 4

    def columns_own(w):
        @pl.when(my_chip != t)
        def _():
            for h in range(2):
                column_copy(w, my_chip, (my_chip // 4 + zl) % 2, h).start()

    def columns_out(w):
        for flip, j in ROTATION:
            to = column_target(flip, j)

            @pl.when(to != my_chip)
            def _():
                for h in range(2):
                    column_copy(w, to, flip, h).start()

        stay = column_stay(w)
        stay.start()
        stays[w] = stay

    stays = {}

    def finish_weight_sends(w):
        for copy in sends[w]:
            copy.wait_send()
        for flip, j in ROTATION:
            for h in range(2):
                column_copy(w, column_target(flip, j), flip, h).wait_send()

    def columns_arrived(w):
        for flip, j in ROTATION:
            f = column_target(flip, j)
            for h in range(2):
                dst = w2.at[
                    w, pl.ds(pl.multiple_of(c * SHARD + h * HALF, HALF), HALF), aligned(f, WIDTH, WIDTH)
                ]
                remote(dst, dst, t_send.at[w, f, h], t_recv.at[w, f, h], sibling).wait_recv()
        mine = w2.at[w, aligned(c, SHARD, SHARD)]
        copy = remote(mine, mine, u_send.at[w], u_recv.at[w], sibling)
        copy.start()
        return copy

    def columns_done(w):
        theirs = w2.at[w, aligned(1 - c, SHARD, SHARD)]
        remote(theirs, theirs, u_send.at[w], u_recv.at[w], sibling).wait_recv()

    def accumulate(w, values):
        pre[w] = jnp.dot(values[:, 0:PAIR], wf[w, 0:PAIR], preferred_element_type=jnp.float32)

        @pl.loop(1, 4)
        def _(i):
            block = aligned(i, PAIR, PAIR)
            pre[w] += jnp.dot(values[:, block], wf[w, block], preferred_element_type=jnp.float32)

    def live_rows(i, size):
        per = MICRO_ROWS // size
        row = lax.broadcasted_iota(jnp.int32, (size, WIDTH), 0) + (i % per) * size
        return (row < counts[0, i // per]).astype(jnp.float32)

    TILE = 64

    gathers = []
    TOP, LOW = MICRO_ROWS, MICRO_ROWS // 2

    def act_ref(a, flip, k, low=0, size=ROWS):
        return af.at[a, pl.ds(low, size), aligned(((zl + flip) % 2) * 4 + (y + k) % 4, WIDTH, WIDTH)]

    def act_move(a, flip, k, to, index, low=0, size=ROWS):
        ref = act_ref(a, flip, k, low, size)
        copy = remote(ref, ref, g_send.at[a, index], g_recv.at[a, index], to)
        copy.start()
        gathers.append(copy)

    def act_arrived(a, flip, k, index, low=0, size=ROWS):
        ref = act_ref(a, flip, k, low, size)
        remote(ref, ref, g_send.at[a, index], g_recv.at[a, index], sibling).wait_recv()

    next_z = device(flip_zl=1)

    def gather_out(a):
        act_move(a, 0, 0, next_z, 0)
        act_move(a, 0, 0, device(dy=1), 1)
        act_move(a, 0, 0, device(dy=3), 2)

    def gather_near(a):
        act_arrived(a, 0, 1, 2)
        act_move(a, 0, 1, device(dy=3), 3, 0, TOP)
        act_move(a, 0, 1, next_z, 5, 0, TOP)
        act_arrived(a, 0, 3, 1)
        act_move(a, 0, 3, device(dy=1), 4, TOP, TOP)
        act_move(a, 0, 3, next_z, 6, 0, TOP)
        act_arrived(a, 1, 0, 0)
        act_move(a, 1, 0, device(dy=1), 8, TOP, TOP)
        act_move(a, 1, 0, device(dy=3), 9, TOP, TOP)

    def gather_far(a):
        act_arrived(a, 0, 2, 3, 0, TOP)
        act_move(a, 0, 2, next_z, 7, 0, TOP)
        act_arrived(a, 1, 1, 9, TOP, TOP)
        act_move(a, 1, 1, device(dy=3), 10, TOP, LOW)
        act_arrived(a, 1, 3, 8, TOP, TOP)
        act_move(a, 1, 3, device(dy=1), 11, TOP + LOW, LOW)

    def gather_done(a):
        act_arrived(a, 0, 2, 4, TOP, TOP)
        act_arrived(a, 1, 1, 5, 0, TOP)
        act_arrived(a, 1, 3, 6, 0, TOP)
        act_arrived(a, 1, 2, 7, 0, TOP)
        act_arrived(a, 1, 2, 10, TOP, LOW)
        act_arrived(a, 1, 2, 11, TOP + LOW, LOW)

    def part_at(p, index):
        if p == GATE:
            return lambda low, size: ov.at[pl.ds(low, size), aligned(index, WIDTH, WIDTH)]
        q = {DOWN: GATE, UP: UP}[p]
        return lambda low, size: wf.at[q, pl.ds(pl.multiple_of(index * SHARD + low, 16), size)]

    def dest(i):
        return ((x + 1 + i // 2) % 4) * 2 + i % 2

    def block_of(p, i, core):
        return part_at(p, dest(i) * 2 + core)(0, SHARD)

    def pair_copy(p, i):
        return remote(block_of(p, i, 1 - c), rs.at[p, i], b_send.at[p, i], b_recv.at[p, i], sibling)

    def grad_partials(p, values, a):
        @pl.loop(0, 4)
        def _(i):
            column = (x + 1 + i) % 4
            part = contract_first(values[:, aligned(column, PAIR, PAIR)], af[a, :, my_cols]).astype(jnp.bfloat16)
            for b in range(4):
                part_at(p, column * 4 + b)(0, SHARD)[...] = part[b * SHARD : (b + 1) * SHARD]
            for half in range(2):
                pair_copy(p, 2 * i + half).start()

    def x_copy(p, i):
        j, half = i // 2 + 1, i % 2
        slot = (3 - j) * 2 + half
        return remote(
            block_of(p, i, c), rx.at[p, slot], b_send.at[p, 8 + i], b_recv.at[p, 8 + slot], device(dx=j)
        )

    STEP = 112

    def pair_sums(p):
        for i in (0, 1, 4, 5, 2, 3):
            pair_copy(p, i).wait_recv()
            at = part_at(p, dest(i) * 2 + c)

            @pl.loop(0, SHARD // STEP)
            def _(s):
                low = pl.multiple_of(s * STEP, STEP)
                ref = at(low, STEP)
                total = ref[...].astype(jnp.float32) + rs[p, i, pl.ds(low, STEP)].astype(jnp.float32)
                ref[...] = total.astype(jnp.bfloat16)

            x_copy(p, i).start()

    def z_copy(p):
        src = part_at(p, (x * 2 + 1 - zh) * 2 + c)(0, SHARD)
        return remote(src, rz.at[p], b_send.at[p, 14], b_recv.at[p, 14], across)

    def x_sums(p):
        for i in (6, 7):
            pair_copy(p, i).wait_recv()
        for slot in range(6):
            remote(
                rx.at[p, slot], rx.at[p, slot], b_send.at[p, 8 + slot], b_recv.at[p, 8 + slot], sibling
            ).wait_recv()

        def total(half, low):
            inner = pl.ds(low, STEP)
            ref = part_at(p, (x * 2 + half) * 2 + c)(low, STEP)
            value = ref[...].astype(jnp.float32) + rs[p, 6 + half, inner].astype(jnp.float32)
            for k in range(3):
                value += rx[p, 2 * k + half, inner].astype(jnp.float32)
            return ref, value

        @pl.loop(0, SHARD // STEP)
        def _(s):
            ref, value = total(1 - zh, pl.multiple_of(s * STEP, STEP))
            ref[...] = value.astype(jnp.bfloat16)

        z_copy(p).start()

        @pl.loop(0, SHARD // STEP)
        def _(s):
            low = pl.multiple_of(s * STEP, STEP)
            pre[p, pl.ds(low, STEP)] = total(zh, low)[1]

    grads = {GATE: gate_grad, UP: up_grad, DOWN: down_grad}
    outs = []

    def z_sums(p):
        z_copy(p).wait_recv()

        @pl.loop(0, SHARD // STEP)
        def _(s):
            inner = aligned(s, STEP, STEP)
            pre[p, inner] += rz[p, inner].astype(jnp.float32)

        copy = pltpu.make_async_copy(pre.at[p, pl.ds(0, SHARD)], grads[p], out_sem.at[p])
        copy.start()
        outs.append(copy)

    BASE = 16 * WIDTH

    def write_out(ref, which):
        for m in range(2):
            src = ov.at[pl.ds(m * MICRO_ROWS, MICRO_ROWS), pl.ds(BASE + which * CHIP, CHIP)]
            copy = pltpu.make_async_copy(src, ref.at[m], out_sem.at[3 + 2 * which + m])
            copy.start()
            outs.append(copy)

    def columns_product(a, w, store):
        def tile(low, size):
            store(low, size, contract_last(af[a], w2[w, pl.ds(low, size)]))

        @pl.loop(0, CHIP // 256)
        def _(n):
            tile(pl.multiple_of(n * 256, 256), 256)

        tile(CHIP // 256 * 256, CHIP % 256)

    def store_mixed(low, size, value):
        ov[:, pl.ds(pl.multiple_of(BASE + low, 128), size)] = value.astype(jnp.bfloat16)

    def store_first(low, size, value):
        acc[:, pl.ds(low, size)] = value

    def store_second(low, size, value):
        total = acc[:, pl.ds(low, size)] + value
        ov[:, pl.ds(pl.multiple_of(BASE + CHIP + low, 128), size)] = total.astype(jnp.bfloat16)

    for w in range(3):
        own[w].wait()
    send_own(GATE)
    send_own(UP)
    for w in range(3):
        columns_own(w)
    from_across(GATE)
    from_neighbours(GATE, 0)
    from_across(UP)
    from_neighbours(UP, 0)
    from_neighbours(GATE, 1)
    from_far(GATE, 0)
    from_far(GATE, 1)
    columns_out(GATE)
    from_neighbours(UP, 1)
    send_own(DOWN)
    from_sibling(GATE)
    for copy in loads[:2]:
        copy.wait()
    accumulate(GATE, av)
    from_far(UP, 0)
    from_far(UP, 1)
    columns_out(UP)
    from_across(DOWN)
    from_sibling(UP)
    accumulate(UP, av)

    @pl.loop(0, ROWS // TILE)
    def _(i):
        rows = aligned(i, TILE, TILE)
        gate_pre, up_pre = pre[GATE, rows], pre[UP, rows]
        value = live_rows(i, TILE) * (gate_pre * jax.nn.sigmoid(gate_pre)) * up_pre
        af[HIDDEN, rows, my_cols] = value.astype(jnp.bfloat16)

    gather_out(HIDDEN)
    from_neighbours(DOWN, 0)
    for copy in loads[2:]:
        copy.wait()
    from_neighbours(DOWN, 1)
    finish_weight_sends(GATE)
    stays[GATE].wait()
    grad_partials(DOWN, ov, HIDDEN)
    from_far(DOWN, 0)
    from_far(DOWN, 1)
    columns_out(DOWN)
    from_sibling(DOWN)
    accumulate(DOWN, ov)

    @pl.loop(0, ROWS // TILE)
    def _(i):
        rows = aligned(i, TILE, TILE)
        gate_pre, up_pre, grad_hidden = pre[GATE, rows], pre[UP, rows], pre[DOWN, rows]
        sigma = jax.nn.sigmoid(gate_pre)
        scaled = live_rows(i, TILE) * grad_hidden
        slope = sigma * (1.0 + gate_pre * (1.0 - sigma))
        af[GGP, rows, my_cols] = (scaled * up_pre * slope).astype(jnp.bfloat16)
        af[GUP, rows, my_cols] = (scaled * (gate_pre * sigma)).astype(jnp.bfloat16)

    gather_out(GGP)
    gather_out(GUP)
    pair_sums(DOWN)
    grad_partials(GATE, av, GGP)
    gather_near(HIDDEN)
    finish_weight_sends(UP)
    stays[UP].wait()
    grad_partials(UP, av, GUP)
    pair_sums(GATE)
    gather_far(HIDDEN)
    pair_sums(UP)
    columns = [columns_arrived(GATE), columns_arrived(UP)]
    x_sums(DOWN)
    gather_near(GGP)
    stays[DOWN].wait()
    columns.append(columns_arrived(DOWN))
    gather_near(GUP)
    gather_done(HIDDEN)
    gather_far(GGP)
    gather_far(GUP)
    columns_done(DOWN)
    columns_product(HIDDEN, DOWN, store_mixed)
    write_out(mixed, 0)
    z_sums(DOWN)
    x_sums(GATE)
    gather_done(GGP)
    columns_done(GATE)
    columns_product(GGP, GATE, store_first)
    x_sums(UP)
    gather_done(GUP)
    columns_done(UP)
    columns_product(GUP, UP, store_second)
    write_out(input_grad, 1)
    z_sums(GATE)
    z_sums(UP)
    finish_weight_sends(DOWN)
    for copy in gathers + columns:
        copy.wait_send()
    for p in range(3):
        for i in range(8):
            pair_copy(p, i).wait_send()
        for i in range(6):
            x_copy(p, i).wait_send()
        z_copy(p).wait_send()
    for copy in outs:
        copy.wait()


def hand_on(*refs):
    sources, targets, held, in_sem, out_sem = refs[:5], refs[5:10], refs[10:15], refs[15], refs[16]
    copies_in = [pltpu.make_async_copy(sources[i], held[i], in_sem.at[i]) for i in range(5)]
    copies_out = [pltpu.make_async_copy(held[i], targets[i], out_sem.at[i]) for i in range(5)]
    for copy in copies_in:
        copy.start()
    for i in range(5):
        copies_in[i].wait()
        copies_out[i].start()
    for copy in copies_out:
        copy.wait()


def local(acts, counts, gate_weight, up_weight, down_weight, out_grad):
    bf16, f32 = jnp.bfloat16, jnp.float32
    dma = pltpu.SemaphoreType.DMA
    anywhere = pl.BlockSpec(memory_space=pl.ANY)
    piece = jax.ShapeDtypeStruct((2, MICRO_ROWS, CHIP), bf16)
    grad = jax.ShapeDtypeStruct((SHARD, WIDTH), f32)
    outs = pl.pallas_call(
        kernel,
        name="expert_layer",
        out_shape=(piece, piece, grad, grad, grad),
        in_specs=[anywhere, pl.BlockSpec(memory_space=pltpu.SMEM)] + [anywhere] * 4,
        out_specs=(anywhere,) * 5,
        scratch_shapes=[
            pltpu.VMEM((ROWS, 8 * CHIP), bf16),
            pltpu.VMEM((ROWS, 8 * CHIP), bf16),
            pltpu.VMEM((3, 8 * CHIP, WIDTH), bf16),
            pltpu.VMEM((3, CHIP, 8 * WIDTH), bf16),
            pltpu.VMEM((3, ROWS, 8 * WIDTH), bf16),
            pltpu.VMEM((3, 8, SHARD, WIDTH), bf16),
            pltpu.VMEM((3, 6, SHARD, WIDTH), bf16),
            pltpu.VMEM((3, SHARD, WIDTH), bf16),
            pltpu.VMEM((3, ROWS, WIDTH), f32),
            pltpu.VMEM((ROWS, CHIP), f32),
            dma((4,)),
            dma((3,)),
            dma((3, 17)),
            dma((3, 17)),
            dma((3, 8, 2)),
            dma((3, 8, 2)),
            dma((3,)),
            dma((3,)),
            dma((3, 12)),
            dma((3, 12)),
            dma((3, 15)),
            dma((3, 15)),
            dma((7,)),
        ],
        compiler_params=pltpu.CompilerParams(
            collective_id=0, has_side_effects=True, vmem_limit_bytes=62 * 2**20
        ),
    )(acts, counts, gate_weight, up_weight, down_weight, out_grad)
    return pl.pallas_call(
        hand_on,
        name="hand_on",
        out_shape=(piece, piece, grad, grad, grad),
        in_specs=[anywhere] * 5,
        out_specs=(anywhere,) * 5,
        scratch_shapes=[pltpu.VMEM(leaf.shape, leaf.dtype) for leaf in (piece, piece, grad, grad, grad)]
        + [dma((5,)), dma((5,))],
    )(*outs)


def solution(mesh):
    placed = (
        P(None, "dp", None),
        P("dp", None),
        P("dp", "tensor"),
        P("dp", "tensor"),
        P("dp", "tensor"),
        P(None, "dp", None),
    )
    return jax.shard_map(
        local,
        mesh=mesh,
        in_specs=placed,
        out_specs=(
            P(None, "dp", "tensor"),
            P(None, "dp", "tensor"),
            P("dp", "tensor"),
            P("dp", "tensor"),
            P("dp", "tensor"),
        ),
        check_vma=False,
    )
```

```python
import jax
import jax.numpy as jnp
from jax import lax
from jax.experimental import pallas as pl
from jax.experimental.pallas import tpu as pltpu
from jax.sharding import PartitionSpec as P

MESH = pl.DeviceIdType.MESH
GATE, UP, DOWN = 0, 1, 2
HIDDEN, GGP, GUP = 0, 1, 2
SHARD = 448
CHIP = 2 * SHARD
HALF = SHARD // 2
PAIR = 2 * CHIP
WIDTH = 256
ROWS = 512
MICRO_ROWS = 256


def aligned(index, size, unit):
    return pl.ds(pl.multiple_of(index * unit, unit), size)


def contract_last(left, right):
    return lax.dot_general(left, right, (((1,), (1,)), ((), ())), preferred_element_type=jnp.float32)


def contract_first(left, right):
    return lax.dot_general(left, right, (((0,), (0,)), ((), ())), preferred_element_type=jnp.float32)


def kernel(
    acts, counts, gate_w, up_w, down_w, out_grad,
    mixed, input_grad, gate_grad, up_grad, down_grad,
    av, ov, wf, w2, af, rs, rx, rz, pre, acc, pd,
    load_sem, own_sem, a_send, a_recv, t_send, t_recv, u_send, u_recv,
    g_send, g_recv, b_send, b_recv, out_sem,
):
    dp, t = lax.axis_index("dp"), lax.axis_index("tensor")
    x, zh, c = dp // 4, (dp // 2) % 2, dp % 2
    zl, y = t // 4, t % 4
    my_chip = x * 2 + zh
    weights = (gate_w, up_w, down_w)

    def device(dx=0, flip_zh=0, flip_c=0, flip_zl=0, dy=0):
        return (
            ((x + dx) % 4) * 4 + ((zh + flip_zh) % 2) * 2 + (c + flip_c) % 2,
            ((zl + flip_zl) % 2) * 4 + (y + dy) % 4,
        )

    def chip_of(r):
        return ((x + r % 4) % 4) * 2 + (zh + r // 4) % 2

    def remote(src, dst, send, recv, to):
        return pltpu.make_async_remote_copy(src, dst, send, recv, device_id=to, device_id_type=MESH)

    sibling = device(flip_c=1)
    across = device(flip_zh=1)
    my_cols = aligned(t, WIDTH, WIDTH)

    barrier = pltpu.get_barrier_semaphore()
    partners = [sibling, across] + [device(dx=j) for j in (1, 2, 3)]
    partners += [device(dy=j) for j in (1, 2, 3)]
    partners += [device(flip_zl=1, dy=j) for j in range(4)]
    partners += [device(flip_zl=1, flip_zh=1, dy=j) for j in range(4)]
    for to in partners:
        pl.semaphore_signal(barrier, inc=1, device_id=to, device_id_type=MESH)

    own = [pltpu.make_async_copy(weights[w], wf.at[w, aligned(dp, SHARD, SHARD)], own_sem.at[w]) for w in range(3)]
    for copy in own:
        copy.start()
    loads = []
    for which, (src, dst) in enumerate(((acts, av), (out_grad, ov))):
        for m in range(2):
            loads.append(
                pltpu.make_async_copy(
                    src.at[m], dst.at[pl.ds(m * MICRO_ROWS, MICRO_ROWS)], load_sem.at[2 * which + m]
                )
            )
    for copy in loads:
        copy.start()
    pl.semaphore_wait(barrier, len(partners))

    sends = {w: [] for w in range(3)}

    def shard_rows(r, core, low=0, size=SHARD):
        return pl.ds(pl.multiple_of((chip_of(r) * 2 + core) * SHARD + low, HALF), size)

    def move(w, r, to, index, low=0, size=SHARD):
        ref = wf.at[w, shard_rows(r, c, low, size)]
        copy = remote(ref, ref, a_send.at[w, index], a_recv.at[w, index], to)
        copy.start()
        sends[w].append(copy)

    def arrived(w, r, index, low=0, size=SHARD, core=None):
        ref = wf.at[w, shard_rows(r, c if core is None else core, low, size)]
        remote(ref, ref, a_send.at[w, index], a_recv.at[w, index], sibling).wait_recv()

    def to_sibling(w, r):
        move(w, r, sibling, 9 + r)

    def send_own(w):
        move(w, 0, across, 0)
        move(w, 0, device(dx=1), 1)
        move(w, 0, device(dx=3), 2)
        to_sibling(w, 0)

    def from_across(w):
        arrived(w, 4, 0)
        move(w, 4, device(dx=1), 3)
        move(w, 4, device(dx=3), 4)
        to_sibling(w, 4)

    def from_neighbours(w, flip):
        arrived(w, 4 * flip + 1, 2 + 2 * flip)
        move(w, 4 * flip + 1, device(dx=3), 5 + 2 * flip, 0, HALF)
        to_sibling(w, 4 * flip + 1)
        arrived(w, 4 * flip + 3, 1 + 2 * flip)
        move(w, 4 * flip + 3, device(dx=1), 6 + 2 * flip, HALF, HALF)
        to_sibling(w, 4 * flip + 3)

    def from_far(w, flip):
        arrived(w, 4 * flip + 2, 5 + 2 * flip, 0, HALF)
        arrived(w, 4 * flip + 2, 6 + 2 * flip, HALF, HALF)
        to_sibling(w, 4 * flip + 2)

    def from_sibling(w):
        for r in range(8):
            arrived(w, r, 9 + r, core=1 - c)

    def column_copy(w, to, cross, h):
        src = wf.at[w, pl.ds(pl.multiple_of((to * 2 + c) * SHARD + h * HALF, HALF), HALF)]
        dst = w2.at[w, pl.ds(pl.multiple_of(c * SHARD + h * HALF, HALF), HALF), my_cols]
        where = (x * 4 + ((zh + h * cross) % 2) * 2 + c, to)
        return remote(src, dst, t_send.at[w, to, h], t_recv.at[w, t, h], where)

    def column_stay(w):
        src = wf.at[w, pl.ds(pl.multiple_of((t * 2 + c) * SHARD, SHARD), SHARD)]
        return pltpu.make_async_copy(src, w2.at[w, aligned(c, SHARD, SHARD), my_cols], t_send.at[w, t, 0])

    ROTATION = ((0, 1), (1, 0), (0, 3), (1, 1), (0, 2), (1, 3), (1, 2))

    def column_target(flip, j):
        return ((zl + flip) % 2) * 4 + (y + j) % 4

    def columns_out(w, relations):
        for r in relations:
            to = chip_of(r)

            @pl.when(to != t)
            def _():
                for h in range(2):
                    column_copy(w, to, (to // 4 + zl) % 2, h).start()

            @pl.when(to == t)
            def _():
                column_stay(w).start()

    def finish_weight_sends(w):
        for copy in sends[w]:
            copy.wait_send()
        for flip, j in ROTATION:
            for h in range(2):
                column_copy(w, column_target(flip, j), flip, h).wait_send()

    def columns_arrived(w):
        for flip, j in ROTATION:
            f = column_target(flip, j)
            for h in range(2):
                dst = w2.at[
                    w, pl.ds(pl.multiple_of(c * SHARD + h * HALF, HALF), HALF), aligned(f, WIDTH, WIDTH)
                ]
                remote(dst, dst, t_send.at[w, f, h], t_recv.at[w, f, h], sibling).wait_recv()
        mine = w2.at[w, aligned(c, SHARD, SHARD)]
        copy = remote(mine, mine, u_send.at[w], u_recv.at[w], sibling)
        copy.start()
        return copy

    def columns_done(w):
        theirs = w2.at[w, aligned(1 - c, SHARD, SHARD)]
        remote(theirs, theirs, u_send.at[w], u_recv.at[w], sibling).wait_recv()

    def accumulate(w, values):
        pre[w] = jnp.dot(values[:, 0:PAIR], wf[w, 0:PAIR], preferred_element_type=jnp.float32)

        @pl.loop(1, 4)
        def _(i):
            block = aligned(i, PAIR, PAIR)
            pre[w] += jnp.dot(values[:, block], wf[w, block], preferred_element_type=jnp.float32)

    def live_rows(i, size):
        per = MICRO_ROWS // size
        row = lax.broadcasted_iota(jnp.int32, (size, WIDTH), 0) + (i % per) * size
        return (row < counts[0, i // per]).astype(jnp.float32)

    TILE = 64

    gathers = []
    TOP, LOW = MICRO_ROWS, MICRO_ROWS // 2

    def act_ref(a, flip, k, low=0, size=ROWS):
        return af.at[a, pl.ds(low, size), aligned(((zl + flip) % 2) * 4 + (y + k) % 4, WIDTH, WIDTH)]

    def act_move(a, flip, k, to, index, low=0, size=ROWS):
        ref = act_ref(a, flip, k, low, size)
        copy = remote(ref, ref, g_send.at[a, index], g_recv.at[a, index], to)
        copy.start()
        gathers.append(copy)

    def act_arrived(a, flip, k, index, low=0, size=ROWS):
        ref = act_ref(a, flip, k, low, size)
        remote(ref, ref, g_send.at[a, index], g_recv.at[a, index], sibling).wait_recv()

    next_z = device(flip_zl=1)

    def gather_out(a):
        act_move(a, 0, 0, next_z, 0)
        act_move(a, 0, 0, device(dy=1), 1)
        act_move(a, 0, 0, device(dy=3), 2)

    def gather_near(a):
        act_arrived(a, 0, 1, 2)
        act_move(a, 0, 1, device(dy=3), 3, 0, TOP)
        act_move(a, 0, 1, next_z, 5, 0, TOP)
        act_arrived(a, 0, 3, 1)
        act_move(a, 0, 3, device(dy=1), 4, TOP, TOP)
        act_move(a, 0, 3, next_z, 6, 0, TOP)
        act_arrived(a, 1, 0, 0)
        act_move(a, 1, 0, device(dy=1), 8, TOP, TOP)
        act_move(a, 1, 0, device(dy=3), 9, TOP, TOP)

    def gather_far(a):
        act_arrived(a, 0, 2, 3, 0, TOP)
        act_move(a, 0, 2, next_z, 7, 0, TOP)
        act_arrived(a, 1, 1, 9, TOP, TOP)
        act_move(a, 1, 1, device(dy=3), 10, TOP, LOW)
        act_arrived(a, 1, 3, 8, TOP, TOP)
        act_move(a, 1, 3, device(dy=1), 11, TOP + LOW, LOW)

    def gather_done(a):
        act_arrived(a, 0, 2, 4, TOP, TOP)
        act_arrived(a, 1, 1, 5, 0, TOP)
        act_arrived(a, 1, 3, 6, 0, TOP)
        act_arrived(a, 1, 2, 7, 0, TOP)
        act_arrived(a, 1, 2, 10, TOP, LOW)
        act_arrived(a, 1, 2, 11, TOP + LOW, LOW)

    def part_at(p, index):
        if p == GATE:
            return lambda low, size: ov.at[pl.ds(low, size), aligned(index, WIDTH, WIDTH)]
        held = pd if p == DOWN else wf.at[GATE]
        return lambda low, size: held.at[pl.ds(pl.multiple_of(index * SHARD + low, 16), size)]

    def dest(i):
        return ((x + 1 + i // 2) % 4) * 2 + i % 2

    def block_of(p, i, core):
        return part_at(p, dest(i) * 2 + core)(0, SHARD)

    def pair_copy(p, i):
        return remote(block_of(p, i, 1 - c), rs.at[p, i], b_send.at[p, i], b_recv.at[p, i], sibling)

    def grad_partials(p, values, a):
        @pl.loop(0, 4)
        def _(i):
            column = (x + 1 + i) % 4
            part = contract_first(values[:, aligned(column, PAIR, PAIR)], af[a, :, my_cols]).astype(jnp.bfloat16)
            for b in range(4):
                part_at(p, column * 4 + b)(0, SHARD)[...] = part[b * SHARD : (b + 1) * SHARD]
            for half in range(2):
                pair_copy(p, 2 * i + half).start()

    def x_copy(p, i):
        j, half = i // 2 + 1, i % 2
        slot = (3 - j) * 2 + half
        return remote(
            block_of(p, i, c), rx.at[p, slot], b_send.at[p, 8 + i], b_recv.at[p, 8 + slot], device(dx=j)
        )

    STEP = 112

    def pair_sums(p):
        for i in (0, 1, 4, 5, 2, 3):
            pair_copy(p, i).wait_recv()
            at = part_at(p, dest(i) * 2 + c)

            @pl.loop(0, SHARD // STEP)
            def _(s):
                low = pl.multiple_of(s * STEP, STEP)
                ref = at(low, STEP)
                total = ref[...].astype(jnp.float32) + rs[p, i, pl.ds(low, STEP)].astype(jnp.float32)
                ref[...] = total.astype(jnp.bfloat16)

            x_copy(p, i).start()

    def z_copy(p):
        src = part_at(p, (x * 2 + 1 - zh) * 2 + c)(0, SHARD)
        return remote(src, rz.at[p], b_send.at[p, 14], b_recv.at[p, 14], across)

    def x_sums(p):
        for i in (6, 7):
            pair_copy(p, i).wait_recv()
        for slot in range(6):
            remote(
                rx.at[p, slot], rx.at[p, slot], b_send.at[p, 8 + slot], b_recv.at[p, 8 + slot], sibling
            ).wait_recv()

        def total(half, low):
            inner = pl.ds(low, STEP)
            ref = part_at(p, (x * 2 + half) * 2 + c)(low, STEP)
            value = ref[...].astype(jnp.float32) + rs[p, 6 + half, inner].astype(jnp.float32)
            for k in range(3):
                value += rx[p, 2 * k + half, inner].astype(jnp.float32)
            return ref, value

        @pl.loop(0, SHARD // STEP)
        def _(s):
            ref, value = total(1 - zh, pl.multiple_of(s * STEP, STEP))
            ref[...] = value.astype(jnp.bfloat16)

        z_copy(p).start()

        @pl.loop(0, SHARD // STEP)
        def _(s):
            low = pl.multiple_of(s * STEP, STEP)
            pre[p, pl.ds(low, STEP)] = total(zh, low)[1]

    grads = {GATE: gate_grad, UP: up_grad, DOWN: down_grad}
    outs = []

    def z_sums(p):
        z_copy(p).wait_recv()

        @pl.loop(0, SHARD // STEP)
        def _(s):
            inner = aligned(s, STEP, STEP)
            pre[p, inner] += rz[p, inner].astype(jnp.float32)

        copy = pltpu.make_async_copy(pre.at[p, pl.ds(0, SHARD)], grads[p], out_sem.at[p])
        copy.start()
        outs.append(copy)

    BASE = 16 * WIDTH

    def write_out(ref, which):
        for m in range(2):
            src = ov.at[pl.ds(m * MICRO_ROWS, MICRO_ROWS), pl.ds(BASE + which * CHIP, CHIP)]
            copy = pltpu.make_async_copy(src, ref.at[m], out_sem.at[3 + 2 * which + m])
            copy.start()
            outs.append(copy)

    def columns_product(a, w, store):
        def tile(low, size):
            store(low, size, contract_last(af[a], w2[w, pl.ds(low, size)]))

        @pl.loop(0, CHIP // 256)
        def _(n):
            tile(pl.multiple_of(n * 256, 256), 256)

        tile(CHIP // 256 * 256, CHIP % 256)

    def store_mixed(low, size, value):
        ov[:, pl.ds(pl.multiple_of(BASE + low, 128), size)] = value.astype(jnp.bfloat16)

    def store_first(low, size, value):
        acc[:, pl.ds(low, size)] = value

    def store_second(low, size, value):
        total = acc[:, pl.ds(low, size)] + value
        ov[:, pl.ds(pl.multiple_of(BASE + CHIP + low, 128), size)] = total.astype(jnp.bfloat16)

    NEAR, FAR = (4, 1, 3), (5, 7, 2, 6)
    for w in range(3):
        own[w].wait()
    send_own(GATE)
    columns_out(GATE, (0,))
    from_across(GATE)
    from_neighbours(GATE, 0)
    send_own(UP)
    columns_out(GATE, NEAR)
    from_neighbours(GATE, 1)
    columns_out(UP, (0,))
    from_across(UP)
    from_far(GATE, 0)
    from_far(GATE, 1)
    columns_out(GATE, FAR)
    from_neighbours(UP, 0)
    send_own(DOWN)
    columns_out(UP, NEAR)
    columns_out(DOWN, (0,))
    from_sibling(GATE)
    for copy in loads[:2]:
        copy.wait()
    accumulate(GATE, av)
    from_neighbours(UP, 1)
    from_across(DOWN)
    from_far(UP, 0)
    from_far(UP, 1)
    columns_out(UP, FAR)
    from_neighbours(DOWN, 0)
    from_sibling(UP)
    accumulate(UP, av)

    @pl.loop(0, ROWS // TILE)
    def _(i):
        rows = aligned(i, TILE, TILE)
        gate_pre, up_pre = pre[GATE, rows], pre[UP, rows]
        value = live_rows(i, TILE) * (gate_pre * jax.nn.sigmoid(gate_pre)) * up_pre
        af[HIDDEN, rows, my_cols] = value.astype(jnp.bfloat16)

    gather_out(HIDDEN)
    columns_out(DOWN, NEAR)
    from_neighbours(DOWN, 1)
    for copy in loads[2:]:
        copy.wait()
    grad_partials(DOWN, ov, HIDDEN)
    from_far(DOWN, 0)
    from_far(DOWN, 1)
    columns_out(DOWN, FAR)
    pair_sums(DOWN)
    from_sibling(DOWN)
    accumulate(DOWN, ov)

    @pl.loop(0, ROWS // TILE)
    def _(i):
        rows = aligned(i, TILE, TILE)
        gate_pre, up_pre, grad_hidden = pre[GATE, rows], pre[UP, rows], pre[DOWN, rows]
        sigma = jax.nn.sigmoid(gate_pre)
        scaled = live_rows(i, TILE) * grad_hidden
        slope = sigma * (1.0 + gate_pre * (1.0 - sigma))
        af[GGP, rows, my_cols] = (scaled * up_pre * slope).astype(jnp.bfloat16)
        af[GUP, rows, my_cols] = (scaled * (gate_pre * sigma)).astype(jnp.bfloat16)

    gather_out(GGP)
    gather_out(GUP)
    grad_partials(GATE, av, GGP)
    finish_weight_sends(GATE)
    column_stay(GATE).wait()
    grad_partials(UP, av, GUP)
    gather_near(HIDDEN)
    pair_sums(GATE)
    gather_far(HIDDEN)
    pair_sums(UP)
    columns = [columns_arrived(GATE)]
    column_stay(UP).wait()
    columns.append(columns_arrived(UP))
    x_sums(DOWN)
    gather_near(GGP)
    column_stay(DOWN).wait()
    columns.append(columns_arrived(DOWN))
    gather_near(GUP)
    gather_far(GGP)
    gather_done(HIDDEN)
    columns_done(DOWN)
    columns_product(HIDDEN, DOWN, store_mixed)
    write_out(mixed, 0)
    gather_far(GUP)
    z_sums(DOWN)
    x_sums(GATE)
    gather_done(GGP)
    columns_done(GATE)
    columns_product(GGP, GATE, store_first)
    x_sums(UP)
    gather_done(GUP)
    columns_done(UP)
    columns_product(GUP, UP, store_second)
    write_out(input_grad, 1)
    z_sums(GATE)
    z_sums(UP)
    finish_weight_sends(UP)
    finish_weight_sends(DOWN)
    for copy in gathers + columns:
        copy.wait_send()
    for p in range(3):
        for i in range(8):
            pair_copy(p, i).wait_send()
        for i in range(6):
            x_copy(p, i).wait_send()
        z_copy(p).wait_send()
    for copy in outs:
        copy.wait()


def hand_on(*refs):
    sources, targets, held, in_sem, out_sem = refs[:5], refs[5:10], refs[10:15], refs[15], refs[16]
    copies_in = [pltpu.make_async_copy(sources[i], held[i], in_sem.at[i]) for i in range(5)]
    copies_out = [pltpu.make_async_copy(held[i], targets[i], out_sem.at[i]) for i in range(5)]
    for copy in copies_in:
        copy.start()
    for i in range(5):
        copies_in[i].wait()
        copies_out[i].start()
    for copy in copies_out:
        copy.wait()


def local(acts, counts, gate_weight, up_weight, down_weight, out_grad):
    bf16, f32 = jnp.bfloat16, jnp.float32
    dma = pltpu.SemaphoreType.DMA
    anywhere = pl.BlockSpec(memory_space=pl.ANY)
    piece = jax.ShapeDtypeStruct((2, MICRO_ROWS, CHIP), bf16)
    grad = jax.ShapeDtypeStruct((SHARD, WIDTH), f32)
    outs = pl.pallas_call(
        kernel,
        name="expert_layer",
        out_shape=(piece, piece, grad, grad, grad),
        in_specs=[anywhere, pl.BlockSpec(memory_space=pltpu.SMEM)] + [anywhere] * 4,
        out_specs=(anywhere,) * 5,
        scratch_shapes=[
            pltpu.VMEM((ROWS, 8 * CHIP), bf16),
            pltpu.VMEM((ROWS, 8 * CHIP), bf16),
            pltpu.VMEM((3, 8 * CHIP, WIDTH), bf16),
            pltpu.VMEM((3, CHIP, 8 * WIDTH), bf16),
            pltpu.VMEM((3, ROWS, 8 * WIDTH), bf16),
            pltpu.VMEM((3, 8, SHARD, WIDTH), bf16),
            pltpu.VMEM((3, 6, SHARD, WIDTH), bf16),
            pltpu.VMEM((3, SHARD, WIDTH), bf16),
            pltpu.VMEM((3, ROWS, WIDTH), f32),
            pltpu.VMEM((ROWS, CHIP), f32),
            pltpu.VMEM((8 * CHIP, WIDTH), bf16),
            dma((4,)),
            dma((3,)),
            dma((3, 17)),
            dma((3, 17)),
            dma((3, 8, 2)),
            dma((3, 8, 2)),
            dma((3,)),
            dma((3,)),
            dma((3, 12)),
            dma((3, 12)),
            dma((3, 15)),
            dma((3, 15)),
            dma((7,)),
        ],
        compiler_params=pltpu.CompilerParams(
            collective_id=0, has_side_effects=True, vmem_limit_bytes=62 * 2**20
        ),
    )(acts, counts, gate_weight, up_weight, down_weight, out_grad)
    return pl.pallas_call(
        hand_on,
        name="hand_on",
        out_shape=(piece, piece, grad, grad, grad),
        in_specs=[anywhere] * 5,
        out_specs=(anywhere,) * 5,
        scratch_shapes=[pltpu.VMEM(leaf.shape, leaf.dtype) for leaf in (piece, piece, grad, grad, grad)]
        + [dma((5,)), dma((5,))],
    )(*outs)


def solution(mesh):
    placed = (
        P(None, "dp", None),
        P("dp", None),
        P("dp", "tensor"),
        P("dp", "tensor"),
        P("dp", "tensor"),
        P(None, "dp", None),
    )
    return jax.shard_map(
        local,
        mesh=mesh,
        in_specs=placed,
        out_specs=(
            P(None, "dp", "tensor"),
            P(None, "dp", "tensor"),
            P("dp", "tensor"),
            P("dp", "tensor"),
            P("dp", "tensor"),
        ),
        check_vma=False,
    )
```

```python
import jax
import jax.numpy as jnp
from jax import lax
from jax.experimental import pallas as pl
from jax.experimental.pallas import tpu as pltpu
from jax.sharding import PartitionSpec as P

MESH = pl.DeviceIdType.MESH
GATE, UP, DOWN = 0, 1, 2
HIDDEN, GGP, GUP = 0, 1, 2
SHARD = 448
CHIP = 2 * SHARD
HALF = SHARD // 2
PAIR = 2 * CHIP
WIDTH = 256
ROWS = 512
MICRO_ROWS = 256


def aligned(index, size, unit):
    return pl.ds(pl.multiple_of(index * unit, unit), size)


def contract_last(left, right):
    return lax.dot_general(left, right, (((1,), (1,)), ((), ())), preferred_element_type=jnp.float32)


def contract_first(left, right):
    return lax.dot_general(left, right, (((0,), (0,)), ((), ())), preferred_element_type=jnp.float32)


def kernel(
    acts, counts, gate_w, up_w, down_w, out_grad,
    mixed, input_grad, gate_grad, up_grad, down_grad,
    av, ov, wf, w2, af, rs, rx, rz, pre, acc, pd,
    load_sem, own_sem, a_send, a_recv, t_send, t_recv, u_send, u_recv, v_send, v_recv,
    g_send, g_recv, b_send, b_recv, out_sem,
):
    dp, t = lax.axis_index("dp"), lax.axis_index("tensor")
    x, zh, c = dp // 4, (dp // 2) % 2, dp % 2
    zl, y = t // 4, t % 4
    my_chip = x * 2 + zh
    weights = (gate_w, up_w, down_w)

    def device(dx=0, flip_zh=0, flip_c=0, flip_zl=0, dy=0):
        return (
            ((x + dx) % 4) * 4 + ((zh + flip_zh) % 2) * 2 + (c + flip_c) % 2,
            ((zl + flip_zl) % 2) * 4 + (y + dy) % 4,
        )

    def chip_of(r):
        return ((x + r % 4) % 4) * 2 + (zh + r // 4) % 2

    def remote(src, dst, send, recv, to):
        return pltpu.make_async_remote_copy(src, dst, send, recv, device_id=to, device_id_type=MESH)

    sibling = device(flip_c=1)
    across = device(flip_zh=1)
    my_cols = aligned(t, WIDTH, WIDTH)

    barrier = pltpu.get_barrier_semaphore()
    partners = [sibling, across] + [device(dx=j) for j in (1, 2, 3)]
    partners += [device(dy=j) for j in (1, 2, 3)]
    partners += [device(flip_zl=1, dy=j) for j in range(4)]
    partners += [device(flip_zl=1, flip_zh=1, dy=j) for j in range(4)]
    for to in partners:
        pl.semaphore_signal(barrier, inc=1, device_id=to, device_id_type=MESH)

    own = [pltpu.make_async_copy(weights[w], wf.at[w, aligned(dp, SHARD, SHARD)], own_sem.at[w]) for w in range(3)]
    for copy in own:
        copy.start()
    loads = []
    for which, (src, dst) in enumerate(((acts, av), (out_grad, ov))):
        for m in range(2):
            loads.append(
                pltpu.make_async_copy(
                    src.at[m], dst.at[pl.ds(m * MICRO_ROWS, MICRO_ROWS)], load_sem.at[2 * which + m]
                )
            )
    for copy in loads:
        copy.start()
    pl.semaphore_wait(barrier, len(partners))

    sends = {w: [] for w in range(3)}

    def shard_rows(r, core, low=0, size=SHARD):
        return pl.ds(pl.multiple_of((chip_of(r) * 2 + core) * SHARD + low, HALF), size)

    def move(w, r, to, index, low=0, size=SHARD):
        ref = wf.at[w, shard_rows(r, c, low, size)]
        copy = remote(ref, ref, a_send.at[w, index], a_recv.at[w, index], to)
        copy.start()
        sends[w].append(copy)

    def arrived(w, r, index, low=0, size=SHARD, core=None):
        ref = wf.at[w, shard_rows(r, c if core is None else core, low, size)]
        remote(ref, ref, a_send.at[w, index], a_recv.at[w, index], sibling).wait_recv()

    def to_sibling(w, r):
        move(w, r, sibling, 9 + r)

    def send_across(w):
        move(w, 0, across, 0)

    def send_own(w):
        move(w, 0, device(dx=1), 1)
        move(w, 0, device(dx=3), 2)
        to_sibling(w, 0)

    def from_across(w):
        arrived(w, 4, 0)
        move(w, 4, device(dx=1), 3)
        move(w, 4, device(dx=3), 4)
        to_sibling(w, 4)

    def from_neighbours(w, flip):
        arrived(w, 4 * flip + 1, 2 + 2 * flip)
        move(w, 4 * flip + 1, device(dx=3), 5 + 2 * flip, 0, HALF)
        to_sibling(w, 4 * flip + 1)
        arrived(w, 4 * flip + 3, 1 + 2 * flip)
        move(w, 4 * flip + 3, device(dx=1), 6 + 2 * flip, HALF, HALF)
        to_sibling(w, 4 * flip + 3)

    def from_far(w, flip):
        arrived(w, 4 * flip + 2, 5 + 2 * flip, 0, HALF)
        arrived(w, 4 * flip + 2, 6 + 2 * flip, HALF, HALF)
        to_sibling(w, 4 * flip + 2)

    def from_sibling(w):
        for r in range(8):
            arrived(w, r, 9 + r, core=1 - c)

    def piece_rows(w, h):
        if w == DOWN:
            return (x % 2) * HALF + h * (HALF // 2), HALF // 2
        return h * HALF, HALF

    def column_rows(w, base, h):
        low, size = piece_rows(w, h)
        return pl.ds(pl.multiple_of(base * SHARD + low, HALF // 2), size)

    def column_copy(w, to, cross, h):
        src = wf.at[w, column_rows(w, to * 2 + c, h)]
        dst = w2.at[w, column_rows(w, c, h), my_cols]
        where = (x * 4 + ((zh + h * cross) % 2) * 2 + c, to)
        return remote(src, dst, t_send.at[w, to, h], t_recv.at[w, t, h], where)

    def column_stay(w):
        low, size = ((x % 2) * HALF, HALF) if w == DOWN else (0, SHARD)
        src = wf.at[w, pl.ds(pl.multiple_of((t * 2 + c) * SHARD + low, HALF), size)]
        dst = w2.at[w, pl.ds(pl.multiple_of(c * SHARD + low, HALF), size), my_cols]
        return pltpu.make_async_copy(src, dst, t_send.at[w, t, 0])

    ROTATION = ((0, 1), (1, 0), (0, 3), (1, 1), (0, 2), (1, 3), (1, 2))

    def column_target(flip, j):
        return ((zl + flip) % 2) * 4 + (y + j) % 4

    def columns_out(w, relations):
        for r in relations:
            to = chip_of(r)

            @pl.when(to != t)
            def _():
                for h in range(2):
                    column_copy(w, to, (to // 4 + zl) % 2, h).start()

            @pl.when(to == t)
            def _():
                column_stay(w).start()

    def finish_weight_sends(w):
        for copy in sends[w]:
            copy.wait_send()
        for flip, j in ROTATION:
            for h in range(2):
                column_copy(w, column_target(flip, j), flip, h).wait_send()

    def columns_in(w):
        column_stay(w).wait()
        for flip, j in ROTATION:
            f = column_target(flip, j)
            for h in range(2):
                dst = w2.at[w, column_rows(w, c, h), aligned(f, WIDTH, WIDTH)]
                remote(dst, dst, t_send.at[w, f, h], t_recv.at[w, f, h], sibling).wait_recv()

    def columns_pair(w):
        mine = w2.at[w, aligned(c, SHARD, SHARD)]
        copy = remote(mine, mine, u_send.at[w], u_recv.at[w], sibling)
        copy.start()
        return copy

    def columns_arrived(w):
        columns_in(w)
        return columns_pair(w)

    def quarter(parity, q):
        low = c * SHARD + parity * HALF + q * (HALF // 2)
        return w2.at[DOWN, pl.ds(pl.multiple_of(low, HALF // 2), HALF // 2)]

    def quarters_out():
        columns_in(DOWN)
        out = []
        for q in range(2):
            ref = quarter(x % 2, q)
            copy = remote(ref, ref, v_send.at[q], v_recv.at[q], device(dx=3 - 2 * q))
            copy.start()
            out.append(copy)
        return out

    def quarters_in():
        for q in range(2):
            ref = quarter(1 - x % 2, q)
            remote(ref, ref, v_send.at[q], v_recv.at[q], sibling).wait_recv()
        return columns_pair(DOWN)

    def columns_done(w):
        theirs = w2.at[w, aligned(1 - c, SHARD, SHARD)]
        remote(theirs, theirs, u_send.at[w], u_recv.at[w], sibling).wait_recv()

    def accumulate(w, values):
        pre[w] = jnp.dot(values[:, 0:PAIR], wf[w, 0:PAIR], preferred_element_type=jnp.float32)

        @pl.loop(1, 4)
        def _(i):
            block = aligned(i, PAIR, PAIR)
            pre[w] += jnp.dot(values[:, block], wf[w, block], preferred_element_type=jnp.float32)

    def live_rows(i, size):
        per = MICRO_ROWS // size
        row = lax.broadcasted_iota(jnp.int32, (size, WIDTH), 0) + (i % per) * size
        return (row < counts[0, i // per]).astype(jnp.float32)

    TILE = 64

    gathers = []
    MIDDLE, TOP = ROWS // 2, 256
    LOW = (ROWS - TOP) // 2

    def act_ref(a, flip, k, low=0, size=ROWS):
        return af.at[a, pl.ds(low, size), aligned(((zl + flip) % 2) * 4 + (y + k) % 4, WIDTH, WIDTH)]

    def act_move(a, flip, k, to, index, low=0, size=ROWS):
        ref = act_ref(a, flip, k, low, size)
        copy = remote(ref, ref, g_send.at[a, index], g_recv.at[a, index], to)
        copy.start()
        gathers.append(copy)

    def act_arrived(a, flip, k, index, low=0, size=ROWS):
        ref = act_ref(a, flip, k, low, size)
        remote(ref, ref, g_send.at[a, index], g_recv.at[a, index], sibling).wait_recv()

    next_z = device(flip_zl=1)

    def gather_out(a):
        act_move(a, 0, 0, next_z, 0)
        act_move(a, 0, 0, device(dy=1), 1)
        act_move(a, 0, 0, device(dy=3), 2)

    def gather_near(a):
        act_arrived(a, 0, 1, 2)
        act_move(a, 0, 1, device(dy=3), 3, 0, MIDDLE)
        act_move(a, 0, 1, next_z, 5, 0, TOP)
        act_arrived(a, 0, 3, 1)
        act_move(a, 0, 3, device(dy=1), 4, MIDDLE, ROWS - MIDDLE)
        act_move(a, 0, 3, next_z, 6, 0, TOP)
        act_arrived(a, 1, 0, 0)
        act_move(a, 1, 0, device(dy=1), 8, TOP, ROWS - TOP)
        act_move(a, 1, 0, device(dy=3), 9, TOP, ROWS - TOP)

    def gather_far(a):
        act_arrived(a, 0, 2, 3, 0, MIDDLE)
        act_move(a, 0, 2, next_z, 7, 0, TOP)
        act_arrived(a, 1, 1, 9, TOP, ROWS - TOP)
        act_move(a, 1, 1, device(dy=3), 10, TOP, LOW)
        act_arrived(a, 1, 3, 8, TOP, ROWS - TOP)
        act_move(a, 1, 3, device(dy=1), 11, TOP + LOW, LOW)

    def gather_done(a):
        act_arrived(a, 0, 2, 4, MIDDLE, ROWS - MIDDLE)
        act_arrived(a, 1, 1, 5, 0, TOP)
        act_arrived(a, 1, 3, 6, 0, TOP)
        act_arrived(a, 1, 2, 7, 0, TOP)
        act_arrived(a, 1, 2, 10, TOP, LOW)
        act_arrived(a, 1, 2, 11, TOP + LOW, LOW)

    def part_at(p, index):
        if p == GATE:
            return lambda low, size: ov.at[pl.ds(low, size), aligned(index, WIDTH, WIDTH)]
        held = pd if p == DOWN else wf.at[GATE]
        return lambda low, size: held.at[pl.ds(pl.multiple_of(index * SHARD + low, 16), size)]

    def dest(i):
        return ((x + 1 + i // 2) % 4) * 2 + i % 2

    def block_of(p, i, core):
        return part_at(p, dest(i) * 2 + core)(0, SHARD)

    def pair_copy(p, i):
        return remote(block_of(p, i, 1 - c), rs.at[p, i], b_send.at[p, i], b_recv.at[p, i], sibling)

    def grad_partials(p, values, a):
        @pl.loop(0, 4)
        def _(i):
            column = (x + 1 + i) % 4
            part = contract_first(values[:, aligned(column, PAIR, PAIR)], af[a, :, my_cols]).astype(jnp.bfloat16)
            for b in range(4):
                part_at(p, column * 4 + b)(0, SHARD)[...] = part[b * SHARD : (b + 1) * SHARD]
            for half in range(2):
                pair_copy(p, 2 * i + half).start()

    def along(s):
        return device(dx=1 + 2 * s)

    def far_copy(p, s, half):
        src = part_at(p, (((x + 2) % 4) * 2 + half) * 2 + c)(s * HALF, HALF)
        index = 8 + 2 * s + half
        return remote(
            src, rx.at[p, 4 + s, pl.ds(half * HALF, HALF)], b_send.at[p, index], b_recv.at[p, index], along(s)
        )

    def near_copy(p, s, half, relayed):
        low = (s if relayed else 1 - s) * HALF
        src = part_at(p, (((x + 1 + 2 * s) % 4) * 2 + half) * 2 + c)(low, HALF)
        index = 12 + 4 * s + 2 * half + relayed
        return remote(
            src, rx.at[p, 2 * s + half, pl.ds(low, HALF)], b_send.at[p, index], b_recv.at[p, index], along(s)
        )

    STEP = 112

    def pair_sums(p):
        for i in (2, 3, 0, 1, 4, 5):
            pair_copy(p, i).wait_recv()
            at = part_at(p, dest(i) * 2 + c)

            @pl.loop(0, SHARD // STEP)
            def _(s):
                low = pl.multiple_of(s * STEP, STEP)
                ref = at(low, STEP)
                total = ref[...].astype(jnp.float32) + rs[p, i, pl.ds(low, STEP)].astype(jnp.float32)
                ref[...] = total.astype(jnp.bfloat16)

            j, half = i // 2 + 1, i % 2
            if j == 2:
                far_copy(p, 0, half).start()
                far_copy(p, 1, half).start()
            else:
                near_copy(p, j // 2, half, 0).start()

    def far_sums(p):
        for half in range(2):
            for s in range(2):
                far_copy(p, s, half).wait_recv()
                at = part_at(p, (((x + 1 + 2 * s) % 4) * 2 + half) * 2 + c)

                @pl.loop(0, HALF // STEP)
                def _(i):
                    low = pl.multiple_of(i * STEP, STEP)
                    ref = at(s * HALF + low, STEP)
                    more = rx[p, 4 + s, pl.ds(half * HALF + low, STEP)]
                    ref[...] = (ref[...].astype(jnp.float32) + more.astype(jnp.float32)).astype(jnp.bfloat16)

                near_copy(p, s, half, 1).start()

    def z_copy(p):
        src = part_at(p, (x * 2 + 1 - zh) * 2 + c)(0, SHARD)
        return remote(src, rz.at[p], b_send.at[p, 20], b_recv.at[p, 20], across)

    def x_sums(p):
        for i in (6, 7):
            pair_copy(p, i).wait_recv()
        for half in range(2):
            for s in range(2):
                for relayed in range(2):
                    near_copy(p, s, half, relayed).wait_recv()

        def total(half, low):
            inner = pl.ds(low, STEP)
            ref = part_at(p, (x * 2 + half) * 2 + c)(low, STEP)
            value = ref[...].astype(jnp.float32) + rs[p, 6 + half, inner].astype(jnp.float32)
            for k in range(2):
                value += rx[p, 2 * k + half, inner].astype(jnp.float32)
            return ref, value

        @pl.loop(0, SHARD // STEP)
        def _(s):
            ref, value = total(1 - zh, pl.multiple_of(s * STEP, STEP))
            ref[...] = value.astype(jnp.bfloat16)

        z_copy(p).start()

        @pl.loop(0, SHARD // STEP)
        def _(s):
            low = pl.multiple_of(s * STEP, STEP)
            pre[p, pl.ds(low, STEP)] = total(zh, low)[1]

    grads = {GATE: gate_grad, UP: up_grad, DOWN: down_grad}
    outs = []

    def z_sums(p):
        z_copy(p).wait_recv()

        @pl.loop(0, SHARD // STEP)
        def _(s):
            inner = aligned(s, STEP, STEP)
            pre[p, inner] += rz[p, inner].astype(jnp.float32)

        copy = pltpu.make_async_copy(pre.at[p, pl.ds(0, SHARD)], grads[p], out_sem.at[p])
        copy.start()
        outs.append(copy)

    BASE = 16 * WIDTH

    def write_out(ref, which):
        for m in range(2):
            src = ov.at[pl.ds(m * MICRO_ROWS, MICRO_ROWS), pl.ds(BASE + which * CHIP, CHIP)]
            copy = pltpu.make_async_copy(src, ref.at[m], out_sem.at[3 + 2 * which + m])
            copy.start()
            outs.append(copy)

    def columns_product(a, w, store):
        def tile(low, size):
            store(low, size, contract_last(af[a], w2[w, pl.ds(low, size)]))

        @pl.loop(0, CHIP // 256)
        def _(n):
            tile(pl.multiple_of(n * 256, 256), 256)

        tile(CHIP // 256 * 256, CHIP % 256)

    def store_mixed(low, size, value):
        ov[:, pl.ds(pl.multiple_of(BASE + low, 128), size)] = value.astype(jnp.bfloat16)

    def store_first(low, size, value):
        acc[:, pl.ds(low, size)] = value

    def store_second(low, size, value):
        total = acc[:, pl.ds(low, size)] + value
        ov[:, pl.ds(pl.multiple_of(BASE + CHIP + low, 128), size)] = total.astype(jnp.bfloat16)

    NEAR, FAR = (4, 1, 3), (5, 7, 2, 6)
    for w in range(3):
        own[w].wait()
    send_across(GATE)
    send_own(GATE)
    send_across(UP)
    send_across(DOWN)
    columns_out(GATE, (0,))
    from_across(GATE)
    from_neighbours(GATE, 0)
    send_own(UP)
    columns_out(GATE, NEAR)
    from_neighbours(GATE, 1)
    columns_out(UP, (0,))
    from_across(UP)
    from_far(GATE, 0)
    from_far(GATE, 1)
    columns_out(GATE, FAR)
    from_neighbours(UP, 0)
    send_own(DOWN)
    columns_out(UP, NEAR)
    from_sibling(GATE)
    for copy in loads[:2]:
        copy.wait()
    accumulate(GATE, av)
    from_neighbours(UP, 1)
    from_across(DOWN)
    from_far(UP, 0)
    from_far(UP, 1)
    columns_out(UP, FAR)
    from_neighbours(DOWN, 0)
    from_sibling(UP)
    accumulate(UP, av)

    @pl.loop(0, ROWS // TILE)
    def _(i):
        rows = aligned(i, TILE, TILE)
        gate_pre, up_pre = pre[GATE, rows], pre[UP, rows]
        value = live_rows(i, TILE) * (gate_pre * jax.nn.sigmoid(gate_pre)) * up_pre
        af[HIDDEN, rows, my_cols] = value.astype(jnp.bfloat16)

    gather_out(HIDDEN)
    from_neighbours(DOWN, 1)
    for copy in loads[2:]:
        copy.wait()
    grad_partials(DOWN, ov, HIDDEN)
    from_far(DOWN, 0)
    from_far(DOWN, 1)
    pair_sums(DOWN)
    from_sibling(DOWN)
    accumulate(DOWN, ov)

    @pl.loop(0, ROWS // TILE)
    def _(i):
        rows = aligned(i, TILE, TILE)
        gate_pre, up_pre, grad_hidden = pre[GATE, rows], pre[UP, rows], pre[DOWN, rows]
        sigma = jax.nn.sigmoid(gate_pre)
        scaled = live_rows(i, TILE) * grad_hidden
        slope = sigma * (1.0 + gate_pre * (1.0 - sigma))
        af[GGP, rows, my_cols] = (scaled * up_pre * slope).astype(jnp.bfloat16)
        af[GUP, rows, my_cols] = (scaled * (gate_pre * sigma)).astype(jnp.bfloat16)

    gather_out(GGP)
    gather_out(GUP)
    columns_out(DOWN, (0,) + NEAR + FAR)
    grad_partials(GATE, av, GGP)
    far_sums(DOWN)
    finish_weight_sends(GATE)
    columns = [columns_arrived(GATE)]
    grad_partials(UP, av, GUP)
    gather_near(HIDDEN)
    pair_sums(GATE)
    gather_far(HIDDEN)
    pair_sums(UP)
    far_sums(GATE)
    gather_near(GGP)
    columns.append(columns_arrived(UP))
    gather_near(GUP)
    x_sums(DOWN)
    far_sums(UP)
    columns += quarters_out()
    gather_far(GGP)
    gather_far(GUP)
    gather_done(HIDDEN)
    z_sums(DOWN)
    x_sums(GATE)
    gather_done(GGP)
    columns_done(GATE)
    columns_product(GGP, GATE, store_first)
    columns.append(quarters_in())
    gather_done(GUP)
    columns_done(UP)
    columns_product(GUP, UP, store_second)
    write_out(input_grad, 1)
    x_sums(UP)
    z_sums(GATE)
    columns_done(DOWN)
    columns_product(HIDDEN, DOWN, store_mixed)
    write_out(mixed, 0)
    z_sums(UP)
    finish_weight_sends(UP)
    finish_weight_sends(DOWN)
    for copy in gathers + columns:
        copy.wait_send()
    for p in range(3):
        for i in range(8):
            pair_copy(p, i).wait_send()
        for half in range(2):
            for s in range(2):
                far_copy(p, s, half).wait_send()
                near_copy(p, s, half, 0).wait_send()
                near_copy(p, s, half, 1).wait_send()
        z_copy(p).wait_send()
    for copy in outs:
        copy.wait()


def hand_on(*refs):
    sources, targets, held, in_sem, out_sem = refs[:5], refs[5:10], refs[10:15], refs[15], refs[16]
    copies_in = [pltpu.make_async_copy(sources[i], held[i], in_sem.at[i]) for i in range(5)]
    copies_out = [pltpu.make_async_copy(held[i], targets[i], out_sem.at[i]) for i in range(5)]
    for copy in copies_in:
        copy.start()
    for i in range(5):
        copies_in[i].wait()
        copies_out[i].start()
    for copy in copies_out:
        copy.wait()


def local(acts, counts, gate_weight, up_weight, down_weight, out_grad):
    bf16, f32 = jnp.bfloat16, jnp.float32
    dma = pltpu.SemaphoreType.DMA
    anywhere = pl.BlockSpec(memory_space=pl.ANY)
    piece = jax.ShapeDtypeStruct((2, MICRO_ROWS, CHIP), bf16)
    grad = jax.ShapeDtypeStruct((SHARD, WIDTH), f32)
    outs = pl.pallas_call(
        kernel,
        name="expert_layer",
        out_shape=(piece, piece, grad, grad, grad),
        in_specs=[anywhere, pl.BlockSpec(memory_space=pltpu.SMEM)] + [anywhere] * 4,
        out_specs=(anywhere,) * 5,
        scratch_shapes=[
            pltpu.VMEM((ROWS, 8 * CHIP), bf16),
            pltpu.VMEM((ROWS, 8 * CHIP), bf16),
            pltpu.VMEM((3, 8 * CHIP, WIDTH), bf16),
            pltpu.VMEM((3, CHIP, 8 * WIDTH), bf16),
            pltpu.VMEM((3, ROWS, 8 * WIDTH), bf16),
            pltpu.VMEM((3, 8, SHARD, WIDTH), bf16),
            pltpu.VMEM((3, 6, SHARD, WIDTH), bf16),
            pltpu.VMEM((3, SHARD, WIDTH), bf16),
            pltpu.VMEM((3, ROWS, WIDTH), f32),
            pltpu.VMEM((ROWS, CHIP), f32),
            pltpu.VMEM((8 * CHIP, WIDTH), bf16),
            dma((4,)),
            dma((3,)),
            dma((3, 17)),
            dma((3, 17)),
            dma((3, 8, 2)),
            dma((3, 8, 2)),
            dma((3,)),
            dma((3,)),
            dma((2,)),
            dma((2,)),
            dma((3, 12)),
            dma((3, 12)),
            dma((3, 21)),
            dma((3, 21)),
            dma((7,)),
        ],
        compiler_params=pltpu.CompilerParams(
            collective_id=0, has_side_effects=True, vmem_limit_bytes=62 * 2**20
        ),
    )(acts, counts, gate_weight, up_weight, down_weight, out_grad)
    return pl.pallas_call(
        hand_on,
        name="hand_on",
        out_shape=(piece, piece, grad, grad, grad),
        in_specs=[anywhere] * 5,
        out_specs=(anywhere,) * 5,
        scratch_shapes=[pltpu.VMEM(leaf.shape, leaf.dtype) for leaf in (piece, piece, grad, grad, grad)]
        + [dma((5,)), dma((5,))],
    )(*outs)


def solution(mesh):
    placed = (
        P(None, "dp", None),
        P("dp", None),
        P("dp", "tensor"),
        P("dp", "tensor"),
        P("dp", "tensor"),
        P(None, "dp", None),
    )
    return jax.shard_map(
        local,
        mesh=mesh,
        in_specs=placed,
        out_specs=(
            P(None, "dp", "tensor"),
            P(None, "dp", "tensor"),
            P("dp", "tensor"),
            P("dp", "tensor"),
            P("dp", "tensor"),
        ),
        check_vma=False,
    )
```

```python
import jax
import jax.numpy as jnp
from jax import lax
from jax.experimental import pallas as pl
from jax.experimental.pallas import tpu as pltpu
from jax.sharding import PartitionSpec as P

MESH = pl.DeviceIdType.MESH
GATE, UP, DOWN = 0, 1, 2
HIDDEN, GGP, GUP = 0, 1, 2
SHARD = 448
CHIP = 2 * SHARD
HALF = SHARD // 2
PAIR = 2 * CHIP
WIDTH = 256
ROWS = 512
MICRO_ROWS = 256


def aligned(index, size, unit):
    return pl.ds(pl.multiple_of(index * unit, unit), size)


def contract_last(left, right):
    return lax.dot_general(left, right, (((1,), (1,)), ((), ())), preferred_element_type=jnp.float32)


def contract_first(left, right):
    return lax.dot_general(left, right, (((0,), (0,)), ((), ())), preferred_element_type=jnp.float32)


def kernel(
    acts, counts, gate_w, up_w, down_w, out_grad,
    mixed, input_grad, gate_grad, up_grad, down_grad,
    av, ov, wf, w2, af, rs, rx, rz, pre, acc, pd,
    load_sem, own_sem, a_send, a_recv, t_send, t_recv, u_send, u_recv, v_send, v_recv,
    g_send, g_recv, b_send, b_recv, out_sem,
):
    dp, t = lax.axis_index("dp"), lax.axis_index("tensor")
    x, zh, c = dp // 4, (dp // 2) % 2, dp % 2
    zl, y = t // 4, t % 4
    my_chip = x * 2 + zh
    weights = (gate_w, up_w, down_w)

    def device(dx=0, flip_zh=0, flip_c=0, flip_zl=0, dy=0):
        return (
            ((x + dx) % 4) * 4 + ((zh + flip_zh) % 2) * 2 + (c + flip_c) % 2,
            ((zl + flip_zl) % 2) * 4 + (y + dy) % 4,
        )

    def chip_of(r):
        return ((x + r % 4) % 4) * 2 + (zh + r // 4) % 2

    def remote(src, dst, send, recv, to):
        return pltpu.make_async_remote_copy(src, dst, send, recv, device_id=to, device_id_type=MESH)

    sibling = device(flip_c=1)
    across = device(flip_zh=1)
    my_cols = aligned(t, WIDTH, WIDTH)

    barrier = pltpu.get_barrier_semaphore()
    partners = [sibling, across] + [device(dx=j) for j in (1, 2, 3)]
    partners += [device(dy=j) for j in (1, 2, 3)]
    partners += [device(flip_zl=1, dy=j) for j in range(4)]
    partners += [device(flip_zl=1, flip_zh=1, dy=j) for j in range(4)]
    for to in partners:
        pl.semaphore_signal(barrier, inc=1, device_id=to, device_id_type=MESH)

    own = [pltpu.make_async_copy(weights[w], wf.at[w, aligned(dp, SHARD, SHARD)], own_sem.at[w]) for w in range(3)]
    for copy in own:
        copy.start()
    loads = []
    for which, (src, dst) in enumerate(((acts, av), (out_grad, ov))):
        for m in range(2):
            loads.append(
                pltpu.make_async_copy(
                    src.at[m], dst.at[pl.ds(m * MICRO_ROWS, MICRO_ROWS)], load_sem.at[2 * which + m]
                )
            )
    for copy in loads:
        copy.start()
    pl.semaphore_wait(barrier, len(partners))

    sends = {w: [] for w in range(3)}

    def shard_rows(r, core, low=0, size=SHARD):
        return pl.ds(pl.multiple_of((chip_of(r) * 2 + core) * SHARD + low, HALF), size)

    def move(w, r, to, index, low=0, size=SHARD):
        ref = wf.at[w, shard_rows(r, c, low, size)]
        copy = remote(ref, ref, a_send.at[w, index], a_recv.at[w, index], to)
        copy.start()
        sends[w].append(copy)

    def arrived(w, r, index, low=0, size=SHARD, core=None):
        ref = wf.at[w, shard_rows(r, c if core is None else core, low, size)]
        remote(ref, ref, a_send.at[w, index], a_recv.at[w, index], sibling).wait_recv()

    def to_sibling(w, r):
        move(w, r, sibling, 9 + r)

    def send_across(w):
        move(w, 0, across, 0)

    def send_own(w):
        move(w, 0, device(dx=1), 1)
        move(w, 0, device(dx=3), 2)
        to_sibling(w, 0)

    def from_across(w):
        arrived(w, 4, 0)
        move(w, 4, device(dx=1), 3)
        move(w, 4, device(dx=3), 4)
        to_sibling(w, 4)

    def from_neighbours(w, flip):
        arrived(w, 4 * flip + 1, 2 + 2 * flip)
        move(w, 4 * flip + 1, device(dx=3), 5 + 2 * flip, 0, HALF)
        to_sibling(w, 4 * flip + 1)
        arrived(w, 4 * flip + 3, 1 + 2 * flip)
        move(w, 4 * flip + 3, device(dx=1), 6 + 2 * flip, HALF, HALF)
        to_sibling(w, 4 * flip + 3)

    def from_far(w, flip):
        arrived(w, 4 * flip + 2, 5 + 2 * flip, 0, HALF)
        arrived(w, 4 * flip + 2, 6 + 2 * flip, HALF, HALF)
        to_sibling(w, 4 * flip + 2)

    def from_sibling(w):
        for r in range(8):
            arrived(w, r, 9 + r, core=1 - c)

    def piece_rows(w, h):
        if w == DOWN:
            return (x % 2) * HALF + h * (HALF // 2), HALF // 2
        return h * HALF, HALF

    def column_rows(w, base, h):
        low, size = piece_rows(w, h)
        return pl.ds(pl.multiple_of(base * SHARD + low, HALF // 2), size)

    def column_copy(w, to, cross, h):
        src = wf.at[w, column_rows(w, to * 2 + c, h)]
        dst = w2.at[w, column_rows(w, c, h), my_cols]
        where = (x * 4 + ((zh + h * cross) % 2) * 2 + c, to)
        return remote(src, dst, t_send.at[w, to, h], t_recv.at[w, t, h], where)

    def column_stay(w):
        low, size = ((x % 2) * HALF, HALF) if w == DOWN else (0, SHARD)
        src = wf.at[w, pl.ds(pl.multiple_of((t * 2 + c) * SHARD + low, HALF), size)]
        dst = w2.at[w, pl.ds(pl.multiple_of(c * SHARD + low, HALF), size), my_cols]
        return pltpu.make_async_copy(src, dst, t_send.at[w, t, 0])

    ROTATION = ((0, 1), (1, 0), (0, 3), (1, 1), (0, 2), (1, 3), (1, 2))

    def column_target(flip, j):
        return ((zl + flip) % 2) * 4 + (y + j) % 4

    def columns_out(w, relations):
        for r in relations:
            to = chip_of(r)

            @pl.when(to != t)
            def _():
                for h in range(2):
                    column_copy(w, to, (to // 4 + zl) % 2, h).start()

            @pl.when(to == t)
            def _():
                column_stay(w).start()

    def finish_weight_sends(w):
        for copy in sends[w]:
            copy.wait_send()
        for flip, j in ROTATION:
            for h in range(2):
                column_copy(w, column_target(flip, j), flip, h).wait_send()

    def columns_in(w):
        column_stay(w).wait()
        for flip, j in ROTATION:
            f = column_target(flip, j)
            for h in range(2):
                dst = w2.at[w, column_rows(w, c, h), aligned(f, WIDTH, WIDTH)]
                remote(dst, dst, t_send.at[w, f, h], t_recv.at[w, f, h], sibling).wait_recv()

    def columns_pair(w):
        mine = w2.at[w, aligned(c, SHARD, SHARD)]
        copy = remote(mine, mine, u_send.at[w], u_recv.at[w], sibling)
        copy.start()
        return copy

    def columns_arrived(w):
        columns_in(w)
        return columns_pair(w)

    def quarter(parity, q):
        low = c * SHARD + parity * HALF + q * (HALF // 2)
        return w2.at[DOWN, pl.ds(pl.multiple_of(low, HALF // 2), HALF // 2)]

    def quarters_out():
        columns_in(DOWN)
        out = []
        for q in range(2):
            ref = quarter(x % 2, q)
            copy = remote(ref, ref, v_send.at[q], v_recv.at[q], device(dx=3 - 2 * q))
            copy.start()
            out.append(copy)
        return out

    def quarters_in():
        for q in range(2):
            ref = quarter(1 - x % 2, q)
            remote(ref, ref, v_send.at[q], v_recv.at[q], sibling).wait_recv()
        return columns_pair(DOWN)

    def columns_done(w):
        theirs = w2.at[w, aligned(1 - c, SHARD, SHARD)]
        remote(theirs, theirs, u_send.at[w], u_recv.at[w], sibling).wait_recv()

    def accumulate(w, values):
        pre[w] = jnp.dot(values[:, 0:PAIR], wf[w, 0:PAIR], preferred_element_type=jnp.float32)

        @pl.loop(1, 4)
        def _(i):
            block = aligned(i, PAIR, PAIR)
            pre[w] += jnp.dot(values[:, block], wf[w, block], preferred_element_type=jnp.float32)

    def live_rows(i, size):
        per = MICRO_ROWS // size
        row = lax.broadcasted_iota(jnp.int32, (size, WIDTH), 0) + (i % per) * size
        return (row < counts[0, i // per]).astype(jnp.float32)

    TILE = 64

    gathers = []
    MIDDLE, TOP = ROWS // 2, 256
    LOW = (ROWS - TOP) // 2

    def act_ref(a, flip, k, low=0, size=ROWS):
        return af.at[a, pl.ds(low, size), aligned(((zl + flip) % 2) * 4 + (y + k) % 4, WIDTH, WIDTH)]

    def act_move(a, flip, k, to, index, low=0, size=ROWS):
        ref = act_ref(a, flip, k, low, size)
        copy = remote(ref, ref, g_send.at[a, index], g_recv.at[a, index], to)
        copy.start()
        gathers.append(copy)

    def act_arrived(a, flip, k, index, low=0, size=ROWS):
        ref = act_ref(a, flip, k, low, size)
        remote(ref, ref, g_send.at[a, index], g_recv.at[a, index], sibling).wait_recv()

    next_z = device(flip_zl=1)

    def gather_out(a):
        act_move(a, 0, 0, next_z, 0)
        act_move(a, 0, 0, device(dy=1), 1)
        act_move(a, 0, 0, device(dy=3), 2)

    def gather_near(a):
        act_arrived(a, 1, 0, 0)
        act_move(a, 1, 0, device(dy=1), 8, TOP, ROWS - TOP)
        act_move(a, 1, 0, device(dy=3), 9, TOP, ROWS - TOP)
        act_arrived(a, 0, 1, 2)
        act_move(a, 0, 1, device(dy=3), 3, 0, MIDDLE)
        act_move(a, 0, 1, next_z, 5, 0, TOP)
        act_arrived(a, 0, 3, 1)
        act_move(a, 0, 3, device(dy=1), 4, MIDDLE, ROWS - MIDDLE)
        act_move(a, 0, 3, next_z, 6, 0, TOP)

    def gather_far(a):
        act_arrived(a, 0, 2, 3, 0, MIDDLE)
        act_move(a, 0, 2, next_z, 7, 0, TOP)
        act_arrived(a, 1, 1, 9, TOP, ROWS - TOP)
        act_move(a, 1, 1, device(dy=3), 10, TOP, LOW)
        act_arrived(a, 1, 3, 8, TOP, ROWS - TOP)
        act_move(a, 1, 3, device(dy=1), 11, TOP + LOW, LOW)

    def gather_done(a):
        act_arrived(a, 0, 2, 4, MIDDLE, ROWS - MIDDLE)
        act_arrived(a, 1, 1, 5, 0, TOP)
        act_arrived(a, 1, 3, 6, 0, TOP)
        act_arrived(a, 1, 2, 7, 0, TOP)
        act_arrived(a, 1, 2, 10, TOP, LOW)
        act_arrived(a, 1, 2, 11, TOP + LOW, LOW)

    def part_at(p, index):
        if p == GATE:
            return lambda low, size: ov.at[pl.ds(low, size), aligned(index, WIDTH, WIDTH)]
        held = pd if p == DOWN else wf.at[GATE]
        return lambda low, size: held.at[pl.ds(pl.multiple_of(index * SHARD + low, 16), size)]

    def dest(i):
        return ((x + 1 + i // 2) % 4) * 2 + i % 2

    def block_of(p, i, core):
        return part_at(p, dest(i) * 2 + core)(0, SHARD)

    def pair_copy(p, i):
        return remote(block_of(p, i, 1 - c), rs.at[p, i], b_send.at[p, i], b_recv.at[p, i], sibling)

    def grad_partials(p, values, a):
        @pl.loop(0, 4)
        def _(i):
            column = (x + 1 + i) % 4
            part = contract_first(values[:, aligned(column, PAIR, PAIR)], af[a, :, my_cols]).astype(jnp.bfloat16)
            for b in range(4):
                part_at(p, column * 4 + b)(0, SHARD)[...] = part[b * SHARD : (b + 1) * SHARD]
            for half in range(2):
                pair_copy(p, 2 * i + half).start()

    def along(s):
        return device(dx=1 + 2 * s)

    def far_copy(p, s, half):
        src = part_at(p, (((x + 2) % 4) * 2 + half) * 2 + c)(s * HALF, HALF)
        index = 8 + 2 * s + half
        return remote(
            src, rx.at[p, 4 + s, pl.ds(half * HALF, HALF)], b_send.at[p, index], b_recv.at[p, index], along(s)
        )

    def near_copy(p, s, half, relayed):
        low = (s if relayed else 1 - s) * HALF
        src = part_at(p, (((x + 1 + 2 * s) % 4) * 2 + half) * 2 + c)(low, HALF)
        index = 12 + 4 * s + 2 * half + relayed
        return remote(
            src, rx.at[p, 2 * s + half, pl.ds(low, HALF)], b_send.at[p, index], b_recv.at[p, index], along(s)
        )

    STEP = 112

    def pair_sums(p):
        for i in (2, 3, 0, 1, 4, 5):
            pair_copy(p, i).wait_recv()
            at = part_at(p, dest(i) * 2 + c)

            @pl.loop(0, SHARD // STEP)
            def _(s):
                low = pl.multiple_of(s * STEP, STEP)
                ref = at(low, STEP)
                total = ref[...].astype(jnp.float32) + rs[p, i, pl.ds(low, STEP)].astype(jnp.float32)
                ref[...] = total.astype(jnp.bfloat16)

            j, half = i // 2 + 1, i % 2
            if j == 2:
                far_copy(p, 0, half).start()
                far_copy(p, 1, half).start()
            else:
                near_copy(p, j // 2, half, 0).start()

    def far_sums(p):
        for half in range(2):
            for s in range(2):
                far_copy(p, s, half).wait_recv()
                at = part_at(p, (((x + 1 + 2 * s) % 4) * 2 + half) * 2 + c)

                @pl.loop(0, HALF // STEP)
                def _(i):
                    low = pl.multiple_of(i * STEP, STEP)
                    ref = at(s * HALF + low, STEP)
                    more = rx[p, 4 + s, pl.ds(half * HALF + low, STEP)]
                    ref[...] = (ref[...].astype(jnp.float32) + more.astype(jnp.float32)).astype(jnp.bfloat16)

                near_copy(p, s, half, 1).start()

    def z_copy(p):
        src = part_at(p, (x * 2 + 1 - zh) * 2 + c)(0, SHARD)
        return remote(src, rz.at[p], b_send.at[p, 20], b_recv.at[p, 20], across)

    def x_sums(p):
        for i in (6, 7):
            pair_copy(p, i).wait_recv()
        for half in range(2):
            for s in range(2):
                for relayed in range(2):
                    near_copy(p, s, half, relayed).wait_recv()

        def total(half, low):
            inner = pl.ds(low, STEP)
            ref = part_at(p, (x * 2 + half) * 2 + c)(low, STEP)
            value = ref[...].astype(jnp.float32) + rs[p, 6 + half, inner].astype(jnp.float32)
            for k in range(2):
                value += rx[p, 2 * k + half, inner].astype(jnp.float32)
            return ref, value

        @pl.loop(0, SHARD // STEP)
        def _(s):
            ref, value = total(1 - zh, pl.multiple_of(s * STEP, STEP))
            ref[...] = value.astype(jnp.bfloat16)

        z_copy(p).start()

        @pl.loop(0, SHARD // STEP)
        def _(s):
            low = pl.multiple_of(s * STEP, STEP)
            pre[p, pl.ds(low, STEP)] = total(zh, low)[1]

    grads = {GATE: gate_grad, UP: up_grad, DOWN: down_grad}
    outs = []

    def z_sums(p):
        z_copy(p).wait_recv()

        @pl.loop(0, SHARD // STEP)
        def _(s):
            inner = aligned(s, STEP, STEP)
            pre[p, inner] += rz[p, inner].astype(jnp.float32)

        copy = pltpu.make_async_copy(pre.at[p, pl.ds(0, SHARD)], grads[p], out_sem.at[p])
        copy.start()
        outs.append(copy)

    BASE = 16 * WIDTH

    def write_out(ref, which):
        for m in range(2):
            src = ov.at[pl.ds(m * MICRO_ROWS, MICRO_ROWS), pl.ds(BASE + which * CHIP, CHIP)]
            copy = pltpu.make_async_copy(src, ref.at[m], out_sem.at[3 + 2 * which + m])
            copy.start()
            outs.append(copy)

    def columns_product(a, w, store):
        def tile(low, size):
            store(low, size, contract_last(af[a], w2[w, pl.ds(low, size)]))

        @pl.loop(0, CHIP // 256)
        def _(n):
            tile(pl.multiple_of(n * 256, 256), 256)

        tile(CHIP // 256 * 256, CHIP % 256)

    def store_mixed(low, size, value):
        ov[:, pl.ds(pl.multiple_of(BASE + low, 128), size)] = value.astype(jnp.bfloat16)

    def store_first(low, size, value):
        acc[:, pl.ds(low, size)] = value

    def store_second(low, size, value):
        total = acc[:, pl.ds(low, size)] + value
        ov[:, pl.ds(pl.multiple_of(BASE + CHIP + low, 128), size)] = total.astype(jnp.bfloat16)

    NEAR, FAR = (4, 1, 3), (5, 7, 2, 6)
    for w in range(3):
        own[w].wait()
    send_across(GATE)
    send_own(GATE)
    send_across(UP)
    send_across(DOWN)
    columns_out(GATE, (0,))
    from_across(GATE)
    from_neighbours(GATE, 0)
    send_own(UP)
    columns_out(GATE, NEAR)
    from_neighbours(GATE, 1)
    columns_out(UP, (0,))
    from_across(UP)
    from_far(GATE, 0)
    from_far(GATE, 1)
    columns_out(GATE, FAR)
    from_neighbours(UP, 0)
    send_own(DOWN)
    columns_out(UP, NEAR)
    from_sibling(GATE)
    for copy in loads[:2]:
        copy.wait()
    accumulate(GATE, av)
    from_neighbours(UP, 1)
    from_across(DOWN)
    from_far(UP, 0)
    from_far(UP, 1)
    columns_out(UP, FAR)
    from_neighbours(DOWN, 0)
    from_sibling(UP)
    accumulate(UP, av)

    @pl.loop(0, ROWS // TILE)
    def _(i):
        rows = aligned(i, TILE, TILE)
        gate_pre, up_pre = pre[GATE, rows], pre[UP, rows]
        value = live_rows(i, TILE) * (gate_pre * jax.nn.sigmoid(gate_pre)) * up_pre
        af[HIDDEN, rows, my_cols] = value.astype(jnp.bfloat16)

    gather_out(HIDDEN)
    from_neighbours(DOWN, 1)
    for copy in loads[2:]:
        copy.wait()
    grad_partials(DOWN, ov, HIDDEN)
    from_far(DOWN, 0)
    from_far(DOWN, 1)
    pair_sums(DOWN)
    from_sibling(DOWN)
    accumulate(DOWN, ov)

    @pl.loop(0, ROWS // TILE)
    def _(i):
        rows = aligned(i, TILE, TILE)
        gate_pre, up_pre, grad_hidden = pre[GATE, rows], pre[UP, rows], pre[DOWN, rows]
        sigma = jax.nn.sigmoid(gate_pre)
        scaled = live_rows(i, TILE) * grad_hidden
        slope = sigma * (1.0 + gate_pre * (1.0 - sigma))
        af[GGP, rows, my_cols] = (scaled * up_pre * slope).astype(jnp.bfloat16)
        af[GUP, rows, my_cols] = (scaled * (gate_pre * sigma)).astype(jnp.bfloat16)

    gather_out(GGP)
    gather_out(GUP)
    grad_partials(GATE, av, GGP)
    far_sums(DOWN)
    gather_near(HIDDEN)
    finish_weight_sends(GATE)
    columns = [columns_arrived(GATE)]
    grad_partials(UP, av, GUP)
    pair_sums(GATE)
    gather_far(HIDDEN)
    gather_near(GGP)
    columns_out(DOWN, (0,) + NEAR + FAR)
    pair_sums(UP)
    gather_near(GUP)
    far_sums(GATE)
    gather_far(GGP)
    columns.append(columns_arrived(UP))
    far_sums(UP)
    gather_far(GUP)
    columns += quarters_out()
    x_sums(DOWN)
    gather_done(HIDDEN)
    z_sums(DOWN)
    x_sums(GATE)
    gather_done(GGP)
    columns_done(GATE)
    columns_product(GGP, GATE, store_first)
    columns.append(quarters_in())
    gather_done(GUP)
    columns_done(UP)
    columns_product(GUP, UP, store_second)
    write_out(input_grad, 1)
    x_sums(UP)
    z_sums(GATE)
    columns_done(DOWN)
    columns_product(HIDDEN, DOWN, store_mixed)
    write_out(mixed, 0)
    z_sums(UP)
    finish_weight_sends(UP)
    finish_weight_sends(DOWN)
    for copy in gathers + columns:
        copy.wait_send()
    for p in range(3):
        for i in range(8):
            pair_copy(p, i).wait_send()
        for half in range(2):
            for s in range(2):
                far_copy(p, s, half).wait_send()
                near_copy(p, s, half, 0).wait_send()
                near_copy(p, s, half, 1).wait_send()
        z_copy(p).wait_send()
    for copy in outs:
        copy.wait()


def hand_on(*refs):
    sources, targets, held, in_sem, out_sem = refs[:5], refs[5:10], refs[10:15], refs[15], refs[16]
    copies_in = [pltpu.make_async_copy(sources[i], held[i], in_sem.at[i]) for i in range(5)]
    copies_out = [pltpu.make_async_copy(held[i], targets[i], out_sem.at[i]) for i in range(5)]
    for copy in copies_in:
        copy.start()
    for i in range(5):
        copies_in[i].wait()
        copies_out[i].start()
    for copy in copies_out:
        copy.wait()


def local(acts, counts, gate_weight, up_weight, down_weight, out_grad):
    bf16, f32 = jnp.bfloat16, jnp.float32
    dma = pltpu.SemaphoreType.DMA
    anywhere = pl.BlockSpec(memory_space=pl.ANY)
    piece = jax.ShapeDtypeStruct((2, MICRO_ROWS, CHIP), bf16)
    grad = jax.ShapeDtypeStruct((SHARD, WIDTH), f32)
    outs = pl.pallas_call(
        kernel,
        name="expert_layer",
        out_shape=(piece, piece, grad, grad, grad),
        in_specs=[anywhere, pl.BlockSpec(memory_space=pltpu.SMEM)] + [anywhere] * 4,
        out_specs=(anywhere,) * 5,
        scratch_shapes=[
            pltpu.VMEM((ROWS, 8 * CHIP), bf16),
            pltpu.VMEM((ROWS, 8 * CHIP), bf16),
            pltpu.VMEM((3, 8 * CHIP, WIDTH), bf16),
            pltpu.VMEM((3, CHIP, 8 * WIDTH), bf16),
            pltpu.VMEM((3, ROWS, 8 * WIDTH), bf16),
            pltpu.VMEM((3, 8, SHARD, WIDTH), bf16),
            pltpu.VMEM((3, 6, SHARD, WIDTH), bf16),
            pltpu.VMEM((3, SHARD, WIDTH), bf16),
            pltpu.VMEM((3, ROWS, WIDTH), f32),
            pltpu.VMEM((ROWS, CHIP), f32),
            pltpu.VMEM((8 * CHIP, WIDTH), bf16),
            dma((4,)),
            dma((3,)),
            dma((3, 17)),
            dma((3, 17)),
            dma((3, 8, 2)),
            dma((3, 8, 2)),
            dma((3,)),
            dma((3,)),
            dma((2,)),
            dma((2,)),
            dma((3, 12)),
            dma((3, 12)),
            dma((3, 21)),
            dma((3, 21)),
            dma((7,)),
        ],
        compiler_params=pltpu.CompilerParams(
            collective_id=0, has_side_effects=True, vmem_limit_bytes=62 * 2**20
        ),
    )(acts, counts, gate_weight, up_weight, down_weight, out_grad)
    return pl.pallas_call(
        hand_on,
        name="hand_on",
        out_shape=(piece, piece, grad, grad, grad),
        in_specs=[anywhere] * 5,
        out_specs=(anywhere,) * 5,
        scratch_shapes=[pltpu.VMEM(leaf.shape, leaf.dtype) for leaf in (piece, piece, grad, grad, grad)]
        + [dma((5,)), dma((5,))],
    )(*outs)


def solution(mesh):
    placed = (
        P(None, "dp", None),
        P("dp", None),
        P("dp", "tensor"),
        P("dp", "tensor"),
        P("dp", "tensor"),
        P(None, "dp", None),
    )
    return jax.shard_map(
        local,
        mesh=mesh,
        in_specs=placed,
        out_specs=(
            P(None, "dp", "tensor"),
            P(None, "dp", "tensor"),
            P("dp", "tensor"),
            P("dp", "tensor"),
            P("dp", "tensor"),
        ),
        check_vma=False,
    )
```

```python
import jax
import jax.numpy as jnp
from jax import lax
from jax.experimental import pallas as pl
from jax.experimental.pallas import tpu as pltpu
from jax.sharding import PartitionSpec as P

MESH = pl.DeviceIdType.MESH
GATE, UP, DOWN = 0, 1, 2
HIDDEN, GGP, GUP = 0, 1, 2
SHARD = 448
CHIP = 2 * SHARD
HALF = SHARD // 2
PAIR = 2 * CHIP
WIDTH = 256
ROWS = 512
MICRO_ROWS = 256


def aligned(index, size, unit):
    return pl.ds(pl.multiple_of(index * unit, unit), size)


def contract_last(left, right):
    return lax.dot_general(left, right, (((1,), (1,)), ((), ())), preferred_element_type=jnp.float32)


def contract_first(left, right):
    return lax.dot_general(left, right, (((0,), (0,)), ((), ())), preferred_element_type=jnp.float32)


def kernel(
    acts, counts, gate_w, up_w, down_w, out_grad,
    mixed, input_grad, gate_grad, up_grad, down_grad,
    av, ov, wf, w2, af, rs, rx, rz, pre, acc, pd,
    load_sem, own_sem, a_send, a_recv, t_send, t_recv, u_send, u_recv, v_send, v_recv,
    g_send, g_recv, b_send, b_recv, out_sem,
):
    dp, t = lax.axis_index("dp"), lax.axis_index("tensor")
    x, zh, c = dp // 4, (dp // 2) % 2, dp % 2
    zl, y = t // 4, t % 4
    my_chip = x * 2 + zh
    weights = (gate_w, up_w, down_w)

    def device(dx=0, flip_zh=0, flip_c=0, flip_zl=0, dy=0):
        return (
            ((x + dx) % 4) * 4 + ((zh + flip_zh) % 2) * 2 + (c + flip_c) % 2,
            ((zl + flip_zl) % 2) * 4 + (y + dy) % 4,
        )

    def chip_of(r):
        return ((x + r % 4) % 4) * 2 + (zh + r // 4) % 2

    def remote(src, dst, send, recv, to):
        return pltpu.make_async_remote_copy(src, dst, send, recv, device_id=to, device_id_type=MESH)

    sibling = device(flip_c=1)
    across = device(flip_zh=1)
    my_cols = aligned(t, WIDTH, WIDTH)

    barrier = pltpu.get_barrier_semaphore()
    partners = [sibling, across] + [device(dx=j) for j in (1, 2, 3)]
    partners += [device(dy=j) for j in (1, 2, 3)]
    partners += [device(flip_zl=1, dy=j) for j in range(4)]
    partners += [device(flip_zl=1, flip_zh=1, dy=j) for j in range(4)]
    for to in partners:
        pl.semaphore_signal(barrier, inc=1, device_id=to, device_id_type=MESH)

    own = [pltpu.make_async_copy(weights[w], wf.at[w, aligned(dp, SHARD, SHARD)], own_sem.at[w]) for w in range(3)]
    for copy in own:
        copy.start()
    loads = []
    for which, (src, dst) in enumerate(((acts, av), (out_grad, ov))):
        for m in range(2):
            loads.append(
                pltpu.make_async_copy(
                    src.at[m], dst.at[pl.ds(m * MICRO_ROWS, MICRO_ROWS)], load_sem.at[2 * which + m]
                )
            )
    for copy in loads:
        copy.start()
    pl.semaphore_wait(barrier, len(partners))

    sends = {w: [] for w in range(3)}

    def shard_rows(r, core, low=0, size=SHARD):
        return pl.ds(pl.multiple_of((chip_of(r) * 2 + core) * SHARD + low, HALF), size)

    def move(w, r, to, index, low=0, size=SHARD):
        ref = wf.at[w, shard_rows(r, c, low, size)]
        copy = remote(ref, ref, a_send.at[w, index], a_recv.at[w, index], to)
        copy.start()
        sends[w].append(copy)

    def arrived(w, r, index, low=0, size=SHARD, core=None):
        ref = wf.at[w, shard_rows(r, c if core is None else core, low, size)]
        remote(ref, ref, a_send.at[w, index], a_recv.at[w, index], sibling).wait_recv()

    def to_sibling(w, r):
        move(w, r, sibling, 9 + r)

    def send_across(w):
        move(w, 0, across, 0)

    def send_own(w):
        move(w, 0, device(dx=1), 1)
        move(w, 0, device(dx=3), 2)
        to_sibling(w, 0)

    def from_across(w):
        arrived(w, 4, 0)
        move(w, 4, device(dx=1), 3)
        move(w, 4, device(dx=3), 4)
        to_sibling(w, 4)

    def from_neighbours(w, flip):
        arrived(w, 4 * flip + 1, 2 + 2 * flip)
        move(w, 4 * flip + 1, device(dx=3), 5 + 2 * flip, 0, HALF)
        to_sibling(w, 4 * flip + 1)
        arrived(w, 4 * flip + 3, 1 + 2 * flip)
        move(w, 4 * flip + 3, device(dx=1), 6 + 2 * flip, HALF, HALF)
        to_sibling(w, 4 * flip + 3)

    def from_far(w, flip):
        arrived(w, 4 * flip + 2, 5 + 2 * flip, 0, HALF)
        arrived(w, 4 * flip + 2, 6 + 2 * flip, HALF, HALF)
        to_sibling(w, 4 * flip + 2)

    def from_sibling(w):
        for r in range(8):
            arrived(w, r, 9 + r, core=1 - c)

    def piece_rows(w, h):
        if w == DOWN:
            return (x % 2) * HALF + h * (HALF // 2), HALF // 2
        return h * HALF, HALF

    def column_rows(w, base, h):
        low, size = piece_rows(w, h)
        return pl.ds(pl.multiple_of(base * SHARD + low, HALF // 2), size)

    def column_copy(w, to, cross, h):
        src = wf.at[w, column_rows(w, to * 2 + c, h)]
        dst = w2.at[w, column_rows(w, c, h), my_cols]
        where = (x * 4 + ((zh + h * cross) % 2) * 2 + c, to)
        return remote(src, dst, t_send.at[w, to, h], t_recv.at[w, t, h], where)

    def column_stay(w):
        low, size = ((x % 2) * HALF, HALF) if w == DOWN else (0, SHARD)
        src = wf.at[w, pl.ds(pl.multiple_of((t * 2 + c) * SHARD + low, HALF), size)]
        dst = w2.at[w, pl.ds(pl.multiple_of(c * SHARD + low, HALF), size), my_cols]
        return pltpu.make_async_copy(src, dst, t_send.at[w, t, 0])

    ROTATION = ((0, 1), (1, 0), (0, 3), (1, 1), (0, 2), (1, 3), (1, 2))

    def column_target(flip, j):
        return ((zl + flip) % 2) * 4 + (y + j) % 4

    def columns_out(w, relations):
        for r in relations:
            to = chip_of(r)

            @pl.when(to != t)
            def _():
                for h in range(2):
                    column_copy(w, to, (to // 4 + zl) % 2, h).start()

            @pl.when(to == t)
            def _():
                column_stay(w).start()

    def finish_weight_sends(w):
        for copy in sends[w]:
            copy.wait_send()
        for flip, j in ROTATION:
            for h in range(2):
                column_copy(w, column_target(flip, j), flip, h).wait_send()

    def columns_in(w):
        column_stay(w).wait()
        for flip, j in ROTATION:
            f = column_target(flip, j)
            for h in range(2):
                dst = w2.at[w, column_rows(w, c, h), aligned(f, WIDTH, WIDTH)]
                remote(dst, dst, t_send.at[w, f, h], t_recv.at[w, f, h], sibling).wait_recv()

    def columns_pair(w):
        mine = w2.at[w, aligned(c, SHARD, SHARD)]
        copy = remote(mine, mine, u_send.at[w], u_recv.at[w], sibling)
        copy.start()
        return copy

    def columns_arrived(w):
        columns_in(w)
        return columns_pair(w)

    def quarter(parity, q):
        low = c * SHARD + parity * HALF + q * (HALF // 2)
        return w2.at[DOWN, pl.ds(pl.multiple_of(low, HALF // 2), HALF // 2)]

    def quarters_out():
        columns_in(DOWN)
        out = []
        for q in range(2):
            ref = quarter(x % 2, q)
            copy = remote(ref, ref, v_send.at[q], v_recv.at[q], device(dx=3 - 2 * q))
            copy.start()
            out.append(copy)
        return out

    def quarters_in():
        for q in range(2):
            ref = quarter(1 - x % 2, q)
            remote(ref, ref, v_send.at[q], v_recv.at[q], sibling).wait_recv()
        return columns_pair(DOWN)

    def columns_done(w):
        theirs = w2.at[w, aligned(1 - c, SHARD, SHARD)]
        remote(theirs, theirs, u_send.at[w], u_recv.at[w], sibling).wait_recv()

    def accumulate(w, values):
        pre[w] = jnp.dot(values[:, 0:PAIR], wf[w, 0:PAIR], preferred_element_type=jnp.float32)

        @pl.loop(1, 4)
        def _(i):
            block = aligned(i, PAIR, PAIR)
            pre[w] += jnp.dot(values[:, block], wf[w, block], preferred_element_type=jnp.float32)

    def live_rows(i, size):
        per = MICRO_ROWS // size
        row = lax.broadcasted_iota(jnp.int32, (size, WIDTH), 0) + (i % per) * size
        return (row < counts[0, i // per]).astype(jnp.float32)

    TILE = 64

    gathers = []
    MIDDLE, TOP = ROWS // 2, 256
    LOW = (ROWS - TOP) // 2

    def act_ref(a, flip, k, low=0, size=ROWS):
        return af.at[a, pl.ds(low, size), aligned(((zl + flip) % 2) * 4 + (y + k) % 4, WIDTH, WIDTH)]

    def act_move(a, flip, k, to, index, low=0, size=ROWS):
        ref = act_ref(a, flip, k, low, size)
        copy = remote(ref, ref, g_send.at[a, index], g_recv.at[a, index], to)
        copy.start()
        gathers.append(copy)

    def act_arrived(a, flip, k, index, low=0, size=ROWS):
        ref = act_ref(a, flip, k, low, size)
        remote(ref, ref, g_send.at[a, index], g_recv.at[a, index], sibling).wait_recv()

    next_z = device(flip_zl=1)

    def gather_out(a):
        act_move(a, 0, 0, next_z, 0)
        act_move(a, 0, 0, device(dy=1), 1)
        act_move(a, 0, 0, device(dy=3), 2)

    def gather_near(a):
        act_arrived(a, 1, 0, 0)
        act_move(a, 1, 0, device(dy=1), 8, TOP, ROWS - TOP)
        act_move(a, 1, 0, device(dy=3), 9, TOP, ROWS - TOP)
        act_arrived(a, 0, 1, 2)
        act_move(a, 0, 1, device(dy=3), 3, 0, MIDDLE)
        act_move(a, 0, 1, next_z, 5, 0, TOP)
        act_arrived(a, 0, 3, 1)
        act_move(a, 0, 3, device(dy=1), 4, MIDDLE, ROWS - MIDDLE)
        act_move(a, 0, 3, next_z, 6, 0, TOP)

    def gather_far(a):
        act_arrived(a, 0, 2, 3, 0, MIDDLE)
        act_move(a, 0, 2, next_z, 7, 0, TOP)
        act_arrived(a, 1, 1, 9, TOP, ROWS - TOP)
        act_move(a, 1, 1, device(dy=3), 10, TOP, LOW)
        act_arrived(a, 1, 3, 8, TOP, ROWS - TOP)
        act_move(a, 1, 3, device(dy=1), 11, TOP + LOW, LOW)

    def gather_done(a):
        act_arrived(a, 0, 2, 4, MIDDLE, ROWS - MIDDLE)
        act_arrived(a, 1, 1, 5, 0, TOP)
        act_arrived(a, 1, 3, 6, 0, TOP)
        act_arrived(a, 1, 2, 7, 0, TOP)
        act_arrived(a, 1, 2, 10, TOP, LOW)
        act_arrived(a, 1, 2, 11, TOP + LOW, LOW)

    def part_at(p, index):
        if p == GATE:
            return lambda low, size: ov.at[pl.ds(low, size), aligned(index, WIDTH, WIDTH)]
        held = pd if p == DOWN else wf.at[GATE]
        return lambda low, size: held.at[pl.ds(pl.multiple_of(index * SHARD + low, 16), size)]

    def dest(i):
        return ((x + 1 + i // 2) % 4) * 2 + i % 2

    def block_of(p, i, core):
        return part_at(p, dest(i) * 2 + core)(0, SHARD)

    def pair_copy(p, i):
        return remote(block_of(p, i, 1 - c), rs.at[p, i], b_send.at[p, i], b_recv.at[p, i], sibling)

    def grad_partials(p, values, a):
        @pl.loop(0, 4)
        def _(i):
            column = (x + 1 + i) % 4
            part = contract_first(values[:, aligned(column, PAIR, PAIR)], af[a, :, my_cols]).astype(jnp.bfloat16)
            for b in range(4):
                part_at(p, column * 4 + b)(0, SHARD)[...] = part[b * SHARD : (b + 1) * SHARD]
            for half in range(2):
                pair_copy(p, 2 * i + half).start()

    def along(s):
        return device(dx=1 + 2 * s)

    def far_copy(p, s, half):
        src = part_at(p, (((x + 2) % 4) * 2 + half) * 2 + c)(s * HALF, HALF)
        index = 8 + 2 * s + half
        return remote(
            src, rx.at[p, 4 + s, pl.ds(half * HALF, HALF)], b_send.at[p, index], b_recv.at[p, index], along(s)
        )

    def near_copy(p, s, half, relayed):
        low = (s if relayed else 1 - s) * HALF
        src = part_at(p, (((x + 1 + 2 * s) % 4) * 2 + half) * 2 + c)(low, HALF)
        index = 12 + 4 * s + 2 * half + relayed
        return remote(
            src, rx.at[p, 2 * s + half, pl.ds(low, HALF)], b_send.at[p, index], b_recv.at[p, index], along(s)
        )

    STEP = 112

    def pair_sums(p):
        for i in (2, 3, 0, 1, 4, 5):
            pair_copy(p, i).wait_recv()
            at = part_at(p, dest(i) * 2 + c)

            @pl.loop(0, SHARD // STEP)
            def _(s):
                low = pl.multiple_of(s * STEP, STEP)
                ref = at(low, STEP)
                total = ref[...].astype(jnp.float32) + rs[p, i, pl.ds(low, STEP)].astype(jnp.float32)
                ref[...] = total.astype(jnp.bfloat16)

            j, half = i // 2 + 1, i % 2
            if j == 2:
                far_copy(p, 0, half).start()
                far_copy(p, 1, half).start()
            else:
                near_copy(p, j // 2, half, 0).start()

    def far_sums(p):
        for half in range(2):
            for s in range(2):
                far_copy(p, s, half).wait_recv()
                at = part_at(p, (((x + 1 + 2 * s) % 4) * 2 + half) * 2 + c)

                @pl.loop(0, HALF // STEP)
                def _(i):
                    low = pl.multiple_of(i * STEP, STEP)
                    ref = at(s * HALF + low, STEP)
                    more = rx[p, 4 + s, pl.ds(half * HALF + low, STEP)]
                    ref[...] = (ref[...].astype(jnp.float32) + more.astype(jnp.float32)).astype(jnp.bfloat16)

                near_copy(p, s, half, 1).start()

    def z_copy(p):
        src = part_at(p, (x * 2 + 1 - zh) * 2 + c)(0, SHARD)
        return remote(src, rz.at[p], b_send.at[p, 20], b_recv.at[p, 20], across)

    def x_sums(p):
        for i in (6, 7):
            pair_copy(p, i).wait_recv()
        for half in range(2):
            for s in range(2):
                for relayed in range(2):
                    near_copy(p, s, half, relayed).wait_recv()

        def total(half, low):
            inner = pl.ds(low, STEP)
            ref = part_at(p, (x * 2 + half) * 2 + c)(low, STEP)
            value = ref[...].astype(jnp.float32) + rs[p, 6 + half, inner].astype(jnp.float32)
            for k in range(2):
                value += rx[p, 2 * k + half, inner].astype(jnp.float32)
            return ref, value

        @pl.loop(0, SHARD // STEP)
        def _(s):
            ref, value = total(1 - zh, pl.multiple_of(s * STEP, STEP))
            ref[...] = value.astype(jnp.bfloat16)

        z_copy(p).start()

        @pl.loop(0, SHARD // STEP)
        def _(s):
            low = pl.multiple_of(s * STEP, STEP)
            pre[p, pl.ds(low, STEP)] = total(zh, low)[1]

    grads = {GATE: gate_grad, UP: up_grad, DOWN: down_grad}
    outs = []

    def z_sums(p):
        z_copy(p).wait_recv()

        @pl.loop(0, SHARD // STEP)
        def _(s):
            inner = aligned(s, STEP, STEP)
            pre[p, inner] += rz[p, inner].astype(jnp.float32)

        copy = pltpu.make_async_copy(pre.at[p, pl.ds(0, SHARD)], grads[p], out_sem.at[p])
        copy.start()
        outs.append(copy)

    BASE = 16 * WIDTH

    def write_out(ref, which):
        for m in range(2):
            src = ov.at[pl.ds(m * MICRO_ROWS, MICRO_ROWS), pl.ds(BASE + which * CHIP, CHIP)]
            copy = pltpu.make_async_copy(src, ref.at[m], out_sem.at[3 + 2 * which + m])
            copy.start()
            outs.append(copy)

    def columns_product(a, w, store):
        def tile(low, size):
            store(low, size, contract_last(af[a], w2[w, pl.ds(low, size)]))

        @pl.loop(0, CHIP // 256)
        def _(n):
            tile(pl.multiple_of(n * 256, 256), 256)

        tile(CHIP // 256 * 256, CHIP % 256)

    def store_mixed(low, size, value):
        ov[:, pl.ds(pl.multiple_of(BASE + low, 128), size)] = value.astype(jnp.bfloat16)

    def store_first(low, size, value):
        acc[:, pl.ds(low, size)] = value

    def store_second(low, size, value):
        total = acc[:, pl.ds(low, size)] + value
        ov[:, pl.ds(pl.multiple_of(BASE + CHIP + low, 128), size)] = total.astype(jnp.bfloat16)

    NEAR, FAR = (4, 1, 3), (5, 7, 2, 6)
    for w in range(3):
        own[w].wait()
    send_across(GATE)
    send_own(GATE)
    send_across(UP)
    send_across(DOWN)
    columns_out(GATE, (0,))
    from_across(GATE)
    from_neighbours(GATE, 0)
    send_own(UP)
    columns_out(GATE, NEAR)
    from_neighbours(GATE, 1)
    columns_out(UP, (0,))
    from_across(UP)
    from_far(GATE, 0)
    from_far(GATE, 1)
    columns_out(GATE, FAR)
    from_neighbours(UP, 0)
    send_own(DOWN)
    columns_out(UP, NEAR)
    from_sibling(GATE)
    for copy in loads[:2]:
        copy.wait()
    accumulate(GATE, av)
    from_neighbours(UP, 1)
    from_across(DOWN)
    from_far(UP, 0)
    from_far(UP, 1)
    columns_out(UP, FAR)
    from_neighbours(DOWN, 0)
    from_sibling(UP)
    accumulate(UP, av)

    @pl.loop(0, ROWS // TILE)
    def _(i):
        rows = aligned(i, TILE, TILE)
        gate_pre, up_pre = pre[GATE, rows], pre[UP, rows]
        value = live_rows(i, TILE) * (gate_pre * jax.nn.sigmoid(gate_pre)) * up_pre
        af[HIDDEN, rows, my_cols] = value.astype(jnp.bfloat16)

    gather_out(HIDDEN)
    from_neighbours(DOWN, 1)
    for copy in loads[2:]:
        copy.wait()
    grad_partials(DOWN, ov, HIDDEN)
    from_far(DOWN, 0)
    from_far(DOWN, 1)
    pair_sums(DOWN)
    from_sibling(DOWN)
    accumulate(DOWN, ov)

    @pl.loop(0, ROWS // TILE)
    def _(i):
        rows = aligned(i, TILE, TILE)
        gate_pre, up_pre, grad_hidden = pre[GATE, rows], pre[UP, rows], pre[DOWN, rows]
        sigma = jax.nn.sigmoid(gate_pre)
        scaled = live_rows(i, TILE) * grad_hidden
        slope = sigma * (1.0 + gate_pre * (1.0 - sigma))
        af[GGP, rows, my_cols] = (scaled * up_pre * slope).astype(jnp.bfloat16)
        af[GUP, rows, my_cols] = (scaled * (gate_pre * sigma)).astype(jnp.bfloat16)

    gather_out(GGP)
    gather_out(GUP)
    grad_partials(GATE, av, GGP)
    far_sums(DOWN)
    gather_near(HIDDEN)
    finish_weight_sends(GATE)
    columns = [columns_arrived(GATE)]
    grad_partials(UP, av, GUP)
    pair_sums(GATE)
    gather_far(HIDDEN)
    gather_near(GGP)
    columns_out(DOWN, (0,) + NEAR + FAR)
    pair_sums(UP)
    gather_near(GUP)
    far_sums(GATE)
    gather_far(GGP)
    columns.append(columns_arrived(UP))
    far_sums(UP)
    gather_far(GUP)
    columns += quarters_out()
    x_sums(DOWN)
    gather_done(HIDDEN)
    z_sums(DOWN)
    x_sums(GATE)
    gather_done(GGP)
    columns_done(GATE)
    columns_product(GGP, GATE, store_first)
    columns.append(quarters_in())
    columns_done(DOWN)
    columns_product(HIDDEN, DOWN, store_mixed)
    write_out(mixed, 0)
    gather_done(GUP)
    columns_done(UP)
    columns_product(GUP, UP, store_second)
    write_out(input_grad, 1)
    x_sums(UP)
    z_sums(GATE)
    z_sums(UP)
    finish_weight_sends(UP)
    finish_weight_sends(DOWN)
    for copy in gathers + columns:
        copy.wait_send()
    for p in range(3):
        for i in range(8):
            pair_copy(p, i).wait_send()
        for half in range(2):
            for s in range(2):
                far_copy(p, s, half).wait_send()
                near_copy(p, s, half, 0).wait_send()
                near_copy(p, s, half, 1).wait_send()
        z_copy(p).wait_send()
    for copy in outs:
        copy.wait()


def hand_on(*refs):
    sources, targets, held, in_sem, out_sem = refs[:5], refs[5:10], refs[10:15], refs[15], refs[16]
    copies_in = [pltpu.make_async_copy(sources[i], held[i], in_sem.at[i]) for i in range(5)]
    copies_out = [pltpu.make_async_copy(held[i], targets[i], out_sem.at[i]) for i in range(5)]
    for copy in copies_in:
        copy.start()
    for i in range(5):
        copies_in[i].wait()
        copies_out[i].start()
    for copy in copies_out:
        copy.wait()


def local(acts, counts, gate_weight, up_weight, down_weight, out_grad):
    bf16, f32 = jnp.bfloat16, jnp.float32
    dma = pltpu.SemaphoreType.DMA
    anywhere = pl.BlockSpec(memory_space=pl.ANY)
    piece = jax.ShapeDtypeStruct((2, MICRO_ROWS, CHIP), bf16)
    grad = jax.ShapeDtypeStruct((SHARD, WIDTH), f32)
    outs = pl.pallas_call(
        kernel,
        name="expert_layer",
        out_shape=(piece, piece, grad, grad, grad),
        in_specs=[anywhere, pl.BlockSpec(memory_space=pltpu.SMEM)] + [anywhere] * 4,
        out_specs=(anywhere,) * 5,
        scratch_shapes=[
            pltpu.VMEM((ROWS, 8 * CHIP), bf16),
            pltpu.VMEM((ROWS, 8 * CHIP), bf16),
            pltpu.VMEM((3, 8 * CHIP, WIDTH), bf16),
            pltpu.VMEM((3, CHIP, 8 * WIDTH), bf16),
            pltpu.VMEM((3, ROWS, 8 * WIDTH), bf16),
            pltpu.VMEM((3, 8, SHARD, WIDTH), bf16),
            pltpu.VMEM((3, 6, SHARD, WIDTH), bf16),
            pltpu.VMEM((3, SHARD, WIDTH), bf16),
            pltpu.VMEM((3, ROWS, WIDTH), f32),
            pltpu.VMEM((ROWS, CHIP), f32),
            pltpu.VMEM((8 * CHIP, WIDTH), bf16),
            dma((4,)),
            dma((3,)),
            dma((3, 17)),
            dma((3, 17)),
            dma((3, 8, 2)),
            dma((3, 8, 2)),
            dma((3,)),
            dma((3,)),
            dma((2,)),
            dma((2,)),
            dma((3, 12)),
            dma((3, 12)),
            dma((3, 21)),
            dma((3, 21)),
            dma((7,)),
        ],
        compiler_params=pltpu.CompilerParams(
            collective_id=0, has_side_effects=True, vmem_limit_bytes=62 * 2**20
        ),
    )(acts, counts, gate_weight, up_weight, down_weight, out_grad)
    return pl.pallas_call(
        hand_on,
        name="hand_on",
        out_shape=(piece, piece, grad, grad, grad),
        in_specs=[anywhere] * 5,
        out_specs=(anywhere,) * 5,
        scratch_shapes=[pltpu.VMEM(leaf.shape, leaf.dtype) for leaf in (piece, piece, grad, grad, grad)]
        + [dma((5,)), dma((5,))],
    )(*outs)


def solution(mesh):
    placed = (
        P(None, "dp", None),
        P("dp", None),
        P("dp", "tensor"),
        P("dp", "tensor"),
        P("dp", "tensor"),
        P(None, "dp", None),
    )
    return jax.shard_map(
        local,
        mesh=mesh,
        in_specs=placed,
        out_specs=(
            P(None, "dp", "tensor"),
            P(None, "dp", "tensor"),
            P("dp", "tensor"),
            P("dp", "tensor"),
            P("dp", "tensor"),
        ),
        check_vma=False,
    )
```

```python
import jax
import jax.numpy as jnp
from jax import lax
from jax.experimental import pallas as pl
from jax.experimental.pallas import tpu as pltpu
from jax.sharding import PartitionSpec as P

MESH = pl.DeviceIdType.MESH
GATE, UP, DOWN = 0, 1, 2
HIDDEN, GGP, GUP = 0, 1, 2
SHARD = 448
CHIP = 2 * SHARD
HALF = SHARD // 2
PAIR = 2 * CHIP
WIDTH = 256
ROWS = 512
MICRO_ROWS = 256


def aligned(index, size, unit):
    return pl.ds(pl.multiple_of(index * unit, unit), size)


def contract_last(left, right):
    return lax.dot_general(left, right, (((1,), (1,)), ((), ())), preferred_element_type=jnp.float32)


def contract_first(left, right):
    return lax.dot_general(left, right, (((0,), (0,)), ((), ())), preferred_element_type=jnp.float32)


def kernel(
    acts, counts, gate_w, up_w, down_w, out_grad,
    mixed, input_grad, gate_grad, up_grad, down_grad,
    av, ov, wf, w2, af, rs, rx, rz, pre, acc, pd,
    load_sem, own_sem, a_send, a_recv, t_send, t_recv, u_send, u_recv, v_send, v_recv,
    g_send, g_recv, b_send, b_recv, out_sem,
):
    dp, t = lax.axis_index("dp"), lax.axis_index("tensor")
    x, zh, c = dp // 4, (dp // 2) % 2, dp % 2
    zl, y = t // 4, t % 4
    my_chip = x * 2 + zh
    weights = (gate_w, up_w, down_w)

    def device(dx=0, flip_zh=0, flip_c=0, flip_zl=0, dy=0):
        return (
            ((x + dx) % 4) * 4 + ((zh + flip_zh) % 2) * 2 + (c + flip_c) % 2,
            ((zl + flip_zl) % 2) * 4 + (y + dy) % 4,
        )

    def chip_of(r):
        return ((x + r % 4) % 4) * 2 + (zh + r // 4) % 2

    def remote(src, dst, send, recv, to):
        return pltpu.make_async_remote_copy(src, dst, send, recv, device_id=to, device_id_type=MESH)

    sibling = device(flip_c=1)
    across = device(flip_zh=1)
    my_cols = aligned(t, WIDTH, WIDTH)

    barrier = pltpu.get_barrier_semaphore()
    partners = [sibling, across] + [device(dx=j) for j in (1, 2, 3)]
    partners += [device(dy=j) for j in (1, 2, 3)]
    partners += [device(flip_zl=1, dy=j) for j in range(4)]
    partners += [device(flip_zl=1, flip_zh=1, dy=j) for j in range(4)]
    for to in partners:
        pl.semaphore_signal(barrier, inc=1, device_id=to, device_id_type=MESH)

    own = [pltpu.make_async_copy(weights[w], wf.at[w, aligned(dp, SHARD, SHARD)], own_sem.at[w]) for w in range(3)]
    for copy in own:
        copy.start()
    loads = []
    for which, (src, dst) in enumerate(((acts, av), (out_grad, ov))):
        for m in range(2):
            loads.append(
                pltpu.make_async_copy(
                    src.at[m], dst.at[pl.ds(m * MICRO_ROWS, MICRO_ROWS)], load_sem.at[2 * which + m]
                )
            )
    for copy in loads:
        copy.start()
    pl.semaphore_wait(barrier, len(partners))

    sends = {w: [] for w in range(3)}

    def shard_rows(r, core, low=0, size=SHARD):
        return pl.ds(pl.multiple_of((chip_of(r) * 2 + core) * SHARD + low, HALF), size)

    def move(w, r, to, index, low=0, size=SHARD):
        ref = wf.at[w, shard_rows(r, c, low, size)]
        copy = remote(ref, ref, a_send.at[w, index], a_recv.at[w, index], to)
        copy.start()
        sends[w].append(copy)

    def arrived(w, r, index, low=0, size=SHARD, core=None):
        ref = wf.at[w, shard_rows(r, c if core is None else core, low, size)]
        remote(ref, ref, a_send.at[w, index], a_recv.at[w, index], sibling).wait_recv()

    def to_sibling(w, r):
        move(w, r, sibling, 9 + r)

    def send_across(w):
        move(w, 0, across, 0)

    def send_own(w):
        move(w, 0, device(dx=1), 1)
        move(w, 0, device(dx=3), 2)
        to_sibling(w, 0)

    def from_across(w):
        arrived(w, 4, 0)
        move(w, 4, device(dx=1), 3)
        move(w, 4, device(dx=3), 4)
        to_sibling(w, 4)

    def from_neighbours(w, flip):
        arrived(w, 4 * flip + 1, 2 + 2 * flip)
        move(w, 4 * flip + 1, device(dx=3), 5 + 2 * flip, 0, HALF)
        to_sibling(w, 4 * flip + 1)
        arrived(w, 4 * flip + 3, 1 + 2 * flip)
        move(w, 4 * flip + 3, device(dx=1), 6 + 2 * flip, HALF, HALF)
        to_sibling(w, 4 * flip + 3)

    def from_far(w, flip):
        arrived(w, 4 * flip + 2, 5 + 2 * flip, 0, HALF)
        arrived(w, 4 * flip + 2, 6 + 2 * flip, HALF, HALF)
        to_sibling(w, 4 * flip + 2)

    def from_sibling(w):
        for r in range(8):
            arrived(w, r, 9 + r, core=1 - c)

    def piece_rows(w, h):
        if w == DOWN:
            return (x % 2) * HALF + h * (HALF // 2), HALF // 2
        return h * HALF, HALF

    def column_rows(w, base, h):
        low, size = piece_rows(w, h)
        return pl.ds(pl.multiple_of(base * SHARD + low, HALF // 2), size)

    def column_copy(w, to, cross, h):
        src = wf.at[w, column_rows(w, to * 2 + c, h)]
        dst = w2.at[w, column_rows(w, c, h), my_cols]
        where = (x * 4 + ((zh + h * cross) % 2) * 2 + c, to)
        return remote(src, dst, t_send.at[w, to, h], t_recv.at[w, t, h], where)

    def column_stay(w):
        low, size = ((x % 2) * HALF, HALF) if w == DOWN else (0, SHARD)
        src = wf.at[w, pl.ds(pl.multiple_of((t * 2 + c) * SHARD + low, HALF), size)]
        dst = w2.at[w, pl.ds(pl.multiple_of(c * SHARD + low, HALF), size), my_cols]
        return pltpu.make_async_copy(src, dst, t_send.at[w, t, 0])

    ROTATION = ((0, 1), (1, 0), (0, 3), (1, 1), (0, 2), (1, 3), (1, 2))

    def column_target(flip, j):
        return ((zl + flip) % 2) * 4 + (y + j) % 4

    def columns_out(w, relations):
        for r in relations:
            to = chip_of(r)

            @pl.when(to != t)
            def _():
                for h in range(2):
                    column_copy(w, to, (to // 4 + zl) % 2, h).start()

            @pl.when(to == t)
            def _():
                column_stay(w).start()

    def finish_weight_sends(w):
        for copy in sends[w]:
            copy.wait_send()
        for flip, j in ROTATION:
            for h in range(2):
                column_copy(w, column_target(flip, j), flip, h).wait_send()

    def columns_in(w):
        column_stay(w).wait()
        for flip, j in ROTATION:
            f = column_target(flip, j)
            for h in range(2):
                dst = w2.at[w, column_rows(w, c, h), aligned(f, WIDTH, WIDTH)]
                remote(dst, dst, t_send.at[w, f, h], t_recv.at[w, f, h], sibling).wait_recv()

    def columns_pair(w):
        mine = w2.at[w, aligned(c, SHARD, SHARD)]
        copy = remote(mine, mine, u_send.at[w], u_recv.at[w], sibling)
        copy.start()
        return copy

    def columns_arrived(w):
        columns_in(w)
        return columns_pair(w)

    def quarter(parity, q):
        low = c * SHARD + parity * HALF + q * (HALF // 2)
        return w2.at[DOWN, pl.ds(pl.multiple_of(low, HALF // 2), HALF // 2)]

    def quarters_out():
        columns_in(DOWN)
        out = []
        for q in range(2):
            ref = quarter(x % 2, q)
            copy = remote(ref, ref, v_send.at[q], v_recv.at[q], device(dx=3 - 2 * q))
            copy.start()
            out.append(copy)
        return out

    def quarters_in():
        for q in range(2):
            ref = quarter(1 - x % 2, q)
            remote(ref, ref, v_send.at[q], v_recv.at[q], sibling).wait_recv()
        return columns_pair(DOWN)

    def columns_done(w):
        theirs = w2.at[w, aligned(1 - c, SHARD, SHARD)]
        remote(theirs, theirs, u_send.at[w], u_recv.at[w], sibling).wait_recv()

    def accumulate(w, values):
        pre[w] = jnp.dot(values[:, 0:PAIR], wf[w, 0:PAIR], preferred_element_type=jnp.float32)

        @pl.loop(1, 4)
        def _(i):
            block = aligned(i, PAIR, PAIR)
            pre[w] += jnp.dot(values[:, block], wf[w, block], preferred_element_type=jnp.float32)

    def live_rows(i, size):
        per = MICRO_ROWS // size
        row = lax.broadcasted_iota(jnp.int32, (size, WIDTH), 0) + (i % per) * size
        return (row < counts[0, i // per]).astype(jnp.float32)

    TILE = 64

    gathers = []
    MIDDLE, TOP = ROWS // 2, 224
    LOW = (ROWS - TOP) // 2

    def act_ref(a, flip, k, low=0, size=ROWS):
        return af.at[a, pl.ds(low, size), aligned(((zl + flip) % 2) * 4 + (y + k) % 4, WIDTH, WIDTH)]

    def act_move(a, flip, k, to, index, low=0, size=ROWS):
        ref = act_ref(a, flip, k, low, size)
        copy = remote(ref, ref, g_send.at[a, index], g_recv.at[a, index], to)
        copy.start()
        gathers.append(copy)

    def act_arrived(a, flip, k, index, low=0, size=ROWS):
        ref = act_ref(a, flip, k, low, size)
        remote(ref, ref, g_send.at[a, index], g_recv.at[a, index], sibling).wait_recv()

    next_z = device(flip_zl=1)

    def gather_out(a):
        act_move(a, 0, 0, next_z, 0)
        act_move(a, 0, 0, device(dy=1), 1)
        act_move(a, 0, 0, device(dy=3), 2)

    def gather_near(a):
        act_arrived(a, 1, 0, 0)
        act_move(a, 1, 0, device(dy=1), 8, TOP, ROWS - TOP)
        act_move(a, 1, 0, device(dy=3), 9, TOP, ROWS - TOP)
        act_arrived(a, 0, 1, 2)
        act_move(a, 0, 1, device(dy=3), 3, 0, MIDDLE)
        act_move(a, 0, 1, next_z, 5, 0, TOP)
        act_arrived(a, 0, 3, 1)
        act_move(a, 0, 3, device(dy=1), 4, MIDDLE, ROWS - MIDDLE)
        act_move(a, 0, 3, next_z, 6, 0, TOP)

    def gather_far(a):
        act_arrived(a, 0, 2, 3, 0, MIDDLE)
        act_move(a, 0, 2, next_z, 7, 0, TOP)
        act_arrived(a, 1, 1, 9, TOP, ROWS - TOP)
        act_move(a, 1, 1, device(dy=3), 10, TOP, LOW)
        act_arrived(a, 1, 3, 8, TOP, ROWS - TOP)
        act_move(a, 1, 3, device(dy=1), 11, TOP + LOW, LOW)

    def gather_done(a):
        act_arrived(a, 0, 2, 4, MIDDLE, ROWS - MIDDLE)
        act_arrived(a, 1, 1, 5, 0, TOP)
        act_arrived(a, 1, 3, 6, 0, TOP)
        act_arrived(a, 1, 2, 7, 0, TOP)
        act_arrived(a, 1, 2, 10, TOP, LOW)
        act_arrived(a, 1, 2, 11, TOP + LOW, LOW)

    def part_at(p, index):
        if p == GATE:
            return lambda low, size: ov.at[pl.ds(low, size), aligned(index, WIDTH, WIDTH)]
        held = pd if p == DOWN else wf.at[GATE]
        return lambda low, size: held.at[pl.ds(pl.multiple_of(index * SHARD + low, 16), size)]

    def dest(i):
        return ((x + 1 + i // 2) % 4) * 2 + i % 2

    def block_of(p, i, core):
        return part_at(p, dest(i) * 2 + core)(0, SHARD)

    def pair_copy(p, i):
        return remote(block_of(p, i, 1 - c), rs.at[p, i], b_send.at[p, i], b_recv.at[p, i], sibling)

    def grad_partials(p, values, a):
        @pl.loop(0, 4)
        def _(i):
            column = (x + 1 + i) % 4
            part = contract_first(values[:, aligned(column, PAIR, PAIR)], af[a, :, my_cols]).astype(jnp.bfloat16)
            for b in range(4):
                part_at(p, column * 4 + b)(0, SHARD)[...] = part[b * SHARD : (b + 1) * SHARD]
            for half in range(2):
                pair_copy(p, 2 * i + half).start()

    def along(s):
        return device(dx=1 + 2 * s)

    def far_copy(p, s, half):
        src = part_at(p, (((x + 2) % 4) * 2 + half) * 2 + c)(s * HALF, HALF)
        index = 8 + 2 * s + half
        return remote(
            src, rx.at[p, 4 + s, pl.ds(half * HALF, HALF)], b_send.at[p, index], b_recv.at[p, index], along(s)
        )

    def near_copy(p, s, half, relayed):
        low = (s if relayed else 1 - s) * HALF
        src = part_at(p, (((x + 1 + 2 * s) % 4) * 2 + half) * 2 + c)(low, HALF)
        index = 12 + 4 * s + 2 * half + relayed
        return remote(
            src, rx.at[p, 2 * s + half, pl.ds(low, HALF)], b_send.at[p, index], b_recv.at[p, index], along(s)
        )

    STEP = 112

    def pair_sums(p):
        for i in (2, 3, 0, 1, 4, 5):
            pair_copy(p, i).wait_recv()
            at = part_at(p, dest(i) * 2 + c)

            @pl.loop(0, SHARD // STEP)
            def _(s):
                low = pl.multiple_of(s * STEP, STEP)
                ref = at(low, STEP)
                total = ref[...].astype(jnp.float32) + rs[p, i, pl.ds(low, STEP)].astype(jnp.float32)
                ref[...] = total.astype(jnp.bfloat16)

            j, half = i // 2 + 1, i % 2
            if j == 2:
                far_copy(p, 0, half).start()
                far_copy(p, 1, half).start()
            else:
                near_copy(p, j // 2, half, 0).start()

    def far_sums(p):
        for half in range(2):
            for s in range(2):
                far_copy(p, s, half).wait_recv()
                at = part_at(p, (((x + 1 + 2 * s) % 4) * 2 + half) * 2 + c)

                @pl.loop(0, HALF // STEP)
                def _(i):
                    low = pl.multiple_of(i * STEP, STEP)
                    ref = at(s * HALF + low, STEP)
                    more = rx[p, 4 + s, pl.ds(half * HALF + low, STEP)]
                    ref[...] = (ref[...].astype(jnp.float32) + more.astype(jnp.float32)).astype(jnp.bfloat16)

                near_copy(p, s, half, 1).start()

    def z_copy(p):
        src = part_at(p, (x * 2 + 1 - zh) * 2 + c)(0, SHARD)
        return remote(src, rz.at[p], b_send.at[p, 20], b_recv.at[p, 20], across)

    def x_sums(p):
        for i in (6, 7):
            pair_copy(p, i).wait_recv()
        for half in range(2):
            for s in range(2):
                for relayed in range(2):
                    near_copy(p, s, half, relayed).wait_recv()

        def total(half, low):
            inner = pl.ds(low, STEP)
            ref = part_at(p, (x * 2 + half) * 2 + c)(low, STEP)
            value = ref[...].astype(jnp.float32) + rs[p, 6 + half, inner].astype(jnp.float32)
            for k in range(2):
                value += rx[p, 2 * k + half, inner].astype(jnp.float32)
            return ref, value

        @pl.loop(0, SHARD // STEP)
        def _(s):
            ref, value = total(1 - zh, pl.multiple_of(s * STEP, STEP))
            ref[...] = value.astype(jnp.bfloat16)

        z_copy(p).start()

        @pl.loop(0, SHARD // STEP)
        def _(s):
            low = pl.multiple_of(s * STEP, STEP)
            pre[p, pl.ds(low, STEP)] = total(zh, low)[1]

    grads = {GATE: gate_grad, UP: up_grad, DOWN: down_grad}
    outs = []

    def z_sums(p):
        z_copy(p).wait_recv()

        @pl.loop(0, SHARD // STEP)
        def _(s):
            inner = aligned(s, STEP, STEP)
            pre[p, inner] += rz[p, inner].astype(jnp.float32)

        copy = pltpu.make_async_copy(pre.at[p, pl.ds(0, SHARD)], grads[p], out_sem.at[p])
        copy.start()
        outs.append(copy)

    BASE = 16 * WIDTH

    def write_out(ref, which):
        for m in range(2):
            src = ov.at[pl.ds(m * MICRO_ROWS, MICRO_ROWS), pl.ds(BASE + which * CHIP, CHIP)]
            copy = pltpu.make_async_copy(src, ref.at[m], out_sem.at[3 + 2 * which + m])
            copy.start()
            outs.append(copy)

    def columns_product(a, w, store):
        def tile(low, size):
            store(low, size, contract_last(af[a], w2[w, pl.ds(low, size)]))

        @pl.loop(0, CHIP // 256)
        def _(n):
            tile(pl.multiple_of(n * 256, 256), 256)

        tile(CHIP // 256 * 256, CHIP % 256)

    def store_mixed(low, size, value):
        ov[:, pl.ds(pl.multiple_of(BASE + low, 128), size)] = value.astype(jnp.bfloat16)

    def store_first(low, size, value):
        acc[:, pl.ds(low, size)] = value

    def store_second(low, size, value):
        total = acc[:, pl.ds(low, size)] + value
        ov[:, pl.ds(pl.multiple_of(BASE + CHIP + low, 128), size)] = total.astype(jnp.bfloat16)

    NEAR, FAR = (4, 1, 3), (5, 7, 2, 6)
    for w in range(3):
        own[w].wait()
    send_across(GATE)
    send_own(GATE)
    send_across(UP)
    send_across(DOWN)
    columns_out(GATE, (0,))
    from_across(GATE)
    from_neighbours(GATE, 0)
    send_own(UP)
    columns_out(GATE, NEAR)
    from_neighbours(GATE, 1)
    columns_out(UP, (0,))
    from_across(UP)
    from_far(GATE, 0)
    from_far(GATE, 1)
    columns_out(GATE, FAR)
    from_neighbours(UP, 0)
    send_own(DOWN)
    columns_out(UP, NEAR)
    from_sibling(GATE)
    for copy in loads[:2]:
        copy.wait()
    accumulate(GATE, av)
    from_neighbours(UP, 1)
    from_across(DOWN)
    from_far(UP, 0)
    from_far(UP, 1)
    columns_out(UP, FAR)
    from_neighbours(DOWN, 0)
    from_sibling(UP)
    accumulate(UP, av)

    @pl.loop(0, ROWS // TILE)
    def _(i):
        rows = aligned(i, TILE, TILE)
        gate_pre, up_pre = pre[GATE, rows], pre[UP, rows]
        value = live_rows(i, TILE) * (gate_pre * jax.nn.sigmoid(gate_pre)) * up_pre
        af[HIDDEN, rows, my_cols] = value.astype(jnp.bfloat16)

    gather_out(HIDDEN)
    from_neighbours(DOWN, 1)
    for copy in loads[2:]:
        copy.wait()
    grad_partials(DOWN, ov, HIDDEN)
    from_far(DOWN, 0)
    from_far(DOWN, 1)
    pair_sums(DOWN)
    from_sibling(DOWN)
    accumulate(DOWN, ov)

    @pl.loop(0, ROWS // TILE)
    def _(i):
        rows = aligned(i, TILE, TILE)
        gate_pre, up_pre, grad_hidden = pre[GATE, rows], pre[UP, rows], pre[DOWN, rows]
        sigma = jax.nn.sigmoid(gate_pre)
        scaled = live_rows(i, TILE) * grad_hidden
        slope = sigma * (1.0 + gate_pre * (1.0 - sigma))
        af[GGP, rows, my_cols] = (scaled * up_pre * slope).astype(jnp.bfloat16)
        af[GUP, rows, my_cols] = (scaled * (gate_pre * sigma)).astype(jnp.bfloat16)

    gather_out(GGP)
    gather_out(GUP)
    grad_partials(GATE, av, GGP)
    far_sums(DOWN)
    gather_near(HIDDEN)
    finish_weight_sends(GATE)
    columns = [columns_arrived(GATE)]
    grad_partials(UP, av, GUP)
    pair_sums(GATE)
    gather_far(HIDDEN)
    gather_near(GGP)
    columns_out(DOWN, (0,) + NEAR + FAR)
    pair_sums(UP)
    gather_near(GUP)
    far_sums(GATE)
    gather_far(GGP)
    columns.append(columns_arrived(UP))
    far_sums(UP)
    gather_far(GUP)
    columns += quarters_out()
    x_sums(DOWN)
    gather_done(HIDDEN)
    z_sums(DOWN)
    x_sums(GATE)
    gather_done(GGP)
    columns_done(GATE)
    columns_product(GGP, GATE, store_first)
    columns.append(quarters_in())
    gather_done(GUP)
    columns_done(UP)
    columns_product(GUP, UP, store_second)
    write_out(input_grad, 1)
    x_sums(UP)
    z_sums(GATE)
    columns_done(DOWN)
    columns_product(HIDDEN, DOWN, store_mixed)
    write_out(mixed, 0)
    z_sums(UP)
    finish_weight_sends(UP)
    finish_weight_sends(DOWN)
    for copy in gathers + columns:
        copy.wait_send()
    for p in range(3):
        for i in range(8):
            pair_copy(p, i).wait_send()
        for half in range(2):
            for s in range(2):
                far_copy(p, s, half).wait_send()
                near_copy(p, s, half, 0).wait_send()
                near_copy(p, s, half, 1).wait_send()
        z_copy(p).wait_send()
    for copy in outs:
        copy.wait()


def hand_on(*refs):
    sources, targets, held, in_sem, out_sem = refs[:5], refs[5:10], refs[10:15], refs[15], refs[16]
    copies_in = [pltpu.make_async_copy(sources[i], held[i], in_sem.at[i]) for i in range(5)]
    copies_out = [pltpu.make_async_copy(held[i], targets[i], out_sem.at[i]) for i in range(5)]
    for copy in copies_in:
        copy.start()
    for i in range(5):
        copies_in[i].wait()
        copies_out[i].start()
    for copy in copies_out:
        copy.wait()


def local(acts, counts, gate_weight, up_weight, down_weight, out_grad):
    bf16, f32 = jnp.bfloat16, jnp.float32
    dma = pltpu.SemaphoreType.DMA
    anywhere = pl.BlockSpec(memory_space=pl.ANY)
    piece = jax.ShapeDtypeStruct((2, MICRO_ROWS, CHIP), bf16)
    grad = jax.ShapeDtypeStruct((SHARD, WIDTH), f32)
    outs = pl.pallas_call(
        kernel,
        name="expert_layer",
        out_shape=(piece, piece, grad, grad, grad),
        in_specs=[anywhere, pl.BlockSpec(memory_space=pltpu.SMEM)] + [anywhere] * 4,
        out_specs=(anywhere,) * 5,
        scratch_shapes=[
            pltpu.VMEM((ROWS, 8 * CHIP), bf16),
            pltpu.VMEM((ROWS, 8 * CHIP), bf16),
            pltpu.VMEM((3, 8 * CHIP, WIDTH), bf16),
            pltpu.VMEM((3, CHIP, 8 * WIDTH), bf16),
            pltpu.VMEM((3, ROWS, 8 * WIDTH), bf16),
            pltpu.VMEM((3, 8, SHARD, WIDTH), bf16),
            pltpu.VMEM((3, 6, SHARD, WIDTH), bf16),
            pltpu.VMEM((3, SHARD, WIDTH), bf16),
            pltpu.VMEM((3, ROWS, WIDTH), f32),
            pltpu.VMEM((ROWS, CHIP), f32),
            pltpu.VMEM((8 * CHIP, WIDTH), bf16),
            dma((4,)),
            dma((3,)),
            dma((3, 17)),
            dma((3, 17)),
            dma((3, 8, 2)),
            dma((3, 8, 2)),
            dma((3,)),
            dma((3,)),
            dma((2,)),
            dma((2,)),
            dma((3, 12)),
            dma((3, 12)),
            dma((3, 21)),
            dma((3, 21)),
            dma((7,)),
        ],
        compiler_params=pltpu.CompilerParams(
            collective_id=0, has_side_effects=True, vmem_limit_bytes=62 * 2**20
        ),
    )(acts, counts, gate_weight, up_weight, down_weight, out_grad)
    return pl.pallas_call(
        hand_on,
        name="hand_on",
        out_shape=(piece, piece, grad, grad, grad),
        in_specs=[anywhere] * 5,
        out_specs=(anywhere,) * 5,
        scratch_shapes=[pltpu.VMEM(leaf.shape, leaf.dtype) for leaf in (piece, piece, grad, grad, grad)]
        + [dma((5,)), dma((5,))],
    )(*outs)


def solution(mesh):
    placed = (
        P(None, "dp", None),
        P("dp", None),
        P("dp", "tensor"),
        P("dp", "tensor"),
        P("dp", "tensor"),
        P(None, "dp", None),
    )
    return jax.shard_map(
        local,
        mesh=mesh,
        in_specs=placed,
        out_specs=(
            P(None, "dp", "tensor"),
            P(None, "dp", "tensor"),
            P("dp", "tensor"),
            P("dp", "tensor"),
            P("dp", "tensor"),
        ),
        check_vma=False,
    )
```
